32 devices in a mesh: grp: 2 (over x), req: 8 (over z, y), head: 2 (over core).
Axes of the slice: x: 2, y: 2, z: 4, core: 2. Of those that a mesh axis runs over, the one named last changes fastest.
Arguments:
- x_rows: bfloat16 [22528, 8192], P(('grp', 'req'), 'head'), parts along dimension 0, may hold values from -6 to 6
- b_rows: bfloat16 [22528, 1024], P(('grp', 'req'), 'head'), parts along dimension 0, may hold values from -0.59765625 to 0.59765625
- c_rows: bfloat16 [22528, 1024], P(('grp', 'req'), 'head'), parts along dimension 0, may hold values from -6 to 6
- time_step: bfloat16 [128, 22528], P('head', ('grp', 'req')), parts along dimension 1, may hold values from 0 to 4
- decay_log: float32 [128], P('head'), may hold values from -3 to 1
- skip_gain: float32 [128], P('head'), may hold values from 0.1 to 1.9
- prompt_lengths: int32 [16], P('grp'), parts along dimension 0, may hold values from 1 to 1408, as said below
- block_lists: int32 [16, 6], P('grp'), parts along dimension 0, may hold values from 0 to 82, as said below
- decode_slot: int32 [16], P('grp'), parts along dimension 0, may hold values from 0 to 11, as said below
- staying: int32 [16], P('grp'), parts along dimension 0, may hold values from 0 to 1, as said below
Outputs:
- layer_out: bfloat16 [12288, 8192], P(('grp', 'req'), 'head'), parts along dimension 0
- kept_states: float32 [16, 128, 64, 128], P(('grp', 'req'), 'head'), parts along dimension 0
- decode_states: float32 [16, 2, 8, 12, 64, 128], P(('grp', 'req'), 'head'), parts along dimension 0
The draws below stay inside these ranges and needn't reach their ends.
There are 2 independent parts, one for each index of `grp`. The reference program is written for one: setup_inputs(seed, part) draws one part's arguments, and reference() takes and returns one part's arrays. A program takes and returns all parts, laid end to end along the dimension named above; an argument that names none is the same for every part. Nothing has to cross between parts.
Inputs may be any that keep to these rules, and one draw needn't show every extreme that they name: `prompt_lengths`: request r fills nb[r] = ceil(length / 128) slots, nb[r] = 6 + e[r] - e[r-1] with whole numbers 0 <= e[r] <= 5, e[-1] = e[7] = 0, e[6] = 5; some request fills all 11 slots. `block_lists`: row p lists the last e[p-1] filled slots of request p-1, then the first 6 - e[p-1] slots of request p, each in order (e as for prompt_lengths); every filled slot is listed once. `decode_slot`: distinct slots; slot 0 and slot 11 are used. `staying`: both values occur.
All inputs are finite; a program needn't handle non-finite values.
Results may differ from the reference program's by a relative error of at most 0.0043.
Values may be sent and summed in bfloat16 or wider, within the bound.
No kernel may reach another device: no remote copies, remote signals or barrier semaphores. Data moves between devices by JAX's collectives and lax.ppermute only.
A program may use at most 128 MiB of HBM per device.

```python
import math
import jax
import jax.numpy as jnp
from jax import lax

SCAN_CHANNELS = 128
P_SIZE = 64
N = 128
GROUPS = 8
TILE_HEIGHT = 128
W = 6
DCAP = 12
DEC_REQ = 8
PER_QUERY_TILES = 11
REQS = 8
DH = 8
DGRP = 1
TOTAL_PLACES = 11264
N_HEAD = 2


def plan_blocks(key):
    nested_counter = jax.random.fold_in(key, 11)
    key_extra, key_owner, key_pad = jax.random.split(nested_counter, 3)
    position = jnp.arange(REQS)
    extra = jax.random.randint(key_extra, (REQS,), 0, W)
    chosen_owner = jax.random.randint(key_owner, (), 1, REQS - 2)
    extra = jnp.where(position == chosen_owner, W - 1, extra)
    extra = jnp.where(position == chosen_owner - 1, 0, extra)
    extra = jnp.where(position == REQS - 1, 0, extra)
    extra = jnp.where(position == REQS - 2, W - 1, extra)
    extra_before = jnp.concatenate([jnp.zeros((1,), jnp.int32), extra[:-1].astype(jnp.int32)])
    block_count = W + extra - extra_before
    padding = jax.random.randint(key_pad, (REQS,), 0, TILE_HEIGHT)
    padding = jnp.where(position == chosen_owner, 0, padding)
    lengths = block_count * TILE_HEIGHT - padding
    column = jnp.arange(W)[None, :]
    left_owner = (position + REQS - 1) % REQS
    left_count = block_count[left_owner]
    from_left = column < extra_before[:, None]
    owner_ids = jnp.where(from_left, left_owner[:, None], position[:, None])
    slot_ids = jnp.where(from_left, left_count[:, None] - extra_before[:, None] + column, column - extra_before[:, None])
    lists = owner_ids * PER_QUERY_TILES + slot_ids
    return (lengths.astype(jnp.int32), lists.astype(jnp.int32))


def draw_prompt_lengths(key, part):
    return plan_blocks(key)[0]


def draw_block_lists(key, part):
    return plan_blocks(key)[1]


def draw_decode_slot(key, part):
    nested_counter = jax.random.fold_in(key, 23)
    key_rank, key_order = jax.random.split(nested_counter)
    total = DGRP * DCAP
    payload_elements = jnp.arange(total)
    ranking = jax.random.permutation(key_rank, total)
    ranking = jnp.where(payload_elements == 0, -2, jnp.where(payload_elements == total - 1, -1, ranking))
    ordered = jnp.argsort(ranking, stable=True)
    chosen = ordered[:REQS]
    shuffle = jax.random.permutation(key_order, REQS)
    return chosen[shuffle].astype(jnp.int32)


def draw_staying(key, part):
    nested_counter = jax.random.fold_in(key, 37)
    key_bits, key_one, key_zero = jax.random.split(nested_counter, 3)
    position = jnp.arange(REQS)
    bits = jax.random.randint(key_bits, (REQS,), 0, 2)
    place_one = jax.random.randint(key_one, (), 0, REQS)
    place_zero = (place_one + 1 + jax.random.randint(key_zero, (), 0, REQS - 1)) % REQS
    bits = jnp.where(position == place_one, 1, bits)
    bits = jnp.where(position == place_zero, 0, bits)
    return bits.astype(jnp.int32)


def draw_decay_log(key, part):
    nested_counter = jax.random.fold_in(key, 31)
    key_kind, key_fast, key_slow = jax.random.split(nested_counter, 3)
    fast_share = 0.5
    fast = jax.random.uniform(key_kind, (SCAN_CHANNELS,)) < fast_share
    fast_log = jax.random.uniform(key_fast, (SCAN_CHANNELS,), minval=math.log(1.33), maxval=math.log(2.2))
    slow_log = jax.random.uniform(key_slow, (SCAN_CHANNELS,), minval=math.log(0.08), maxval=math.log(0.12))
    return jnp.where(fast, fast_log, slow_log).astype(jnp.float32)


def draw_time_step(key, part):
    nested_counter = jax.random.fold_in(key, 43)
    starting_random_stream, spike_random_stream, extent_random_stream = jax.random.split(nested_counter, 3)
    starting_shift_amount = 0.015 * jnp.exp(jax.random.uniform(starting_random_stream, (SCAN_CHANNELS, TOTAL_PLACES), minval=-0.7, maxval=0.7))
    spike_lines = jax.random.uniform(spike_random_stream, (TOTAL_PLACES,)) < 2.0 / (PER_QUERY_TILES * TILE_HEIGHT)
    spike_span = jax.random.uniform(extent_random_stream, (SCAN_CHANNELS, TOTAL_PLACES), minval=2.5, maxval=3.5)
    payload_elements = jnp.where(spike_lines[None, :], spike_span, starting_shift_amount)
    return payload_elements.astype(jnp.float32).astype(jnp.bfloat16)


def levels(own_key, shape, shards, least, largest):
    factor_of, own = 1.0, jax.random.fold_in(own_key, 6)
    for axis_at, parts in shards:
        heights = jnp.exp(jax.random.uniform(jax.random.fold_in(own, axis_at), (parts,), jnp.float32, least / len(shards), largest / len(shards)))
        factor_of = factor_of * jnp.repeat(heights, shape[axis_at] // parts).reshape([-1 if axis == axis_at else 1 for axis in range(len(shape))])
    return factor_of


def normal_values(stream_key, dims, scale, most, pieces=(), held_as=jnp.bfloat16):
    values = scale * jax.random.normal(stream_key, dims, jnp.float32)
    if pieces:
        values = values * levels(stream_key, dims, pieces, -0.22, 0.18)
    return jnp.clip(values, -most, most).astype(held_as)


def setup_inputs(seed: int = 0, part: int = 0) -> dict:
    streams_of = jax.random.split(jax.random.key(seed), 11)
    part_splits = jax.random.split(jax.random.fold_in(streams_of[10], part), 11)
    x_rows = normal_values(part_splits[0], (TOTAL_PLACES, SCAN_CHANNELS * P_SIZE), 1.0, 6.0, ((0, 8), (1, 2)))
    b_rows = normal_values(part_splits[1], (TOTAL_PLACES, GROUPS * N), 0.1, 0.59765625, ((0, 8), (1, 2)))
    c_rows = normal_values(part_splits[2], (TOTAL_PLACES, GROUPS * N), 1.0, 6.0, ((0, 8), (1, 2)))
    time_step = draw_time_step(jax.random.fold_in(jax.random.fold_in(streams_of[10], part), 71), part)
    decay_log = draw_decay_log(jax.random.fold_in(streams_of[10], 71), part)
    skip_gain = jnp.clip(1.0 + 0.18 * jax.random.normal(streams_of[5], (SCAN_CHANNELS,), jnp.float32), 0.1, 1.9)
    prompt_lengths = draw_prompt_lengths(jax.random.fold_in(jax.random.fold_in(streams_of[10], part), 71), part)
    block_lists = draw_block_lists(jax.random.fold_in(jax.random.fold_in(streams_of[10], part), 71), part)
    decode_slot = draw_decode_slot(jax.random.fold_in(jax.random.fold_in(streams_of[10], part), 71), part)
    staying = draw_staying(jax.random.fold_in(jax.random.fold_in(streams_of[10], part), 71), part)
    return {"x_rows": x_rows, "b_rows": b_rows, "c_rows": c_rows, "time_step": time_step, "decay_log": decay_log, "skip_gain": skip_gain, "prompt_lengths": prompt_lengths, "block_lists": block_lists, "decode_slot": decode_slot, "staying": staying}


exact_prec = lax.Precision.HIGHEST


def block_step(x_block, b_block, c_block, step_raw, live_rows, decay_rate, skip_value, state_in):
    head_count = decay_rate.shape[0]
    row_count = live_rows.shape[0]
    group_count = b_block.shape[1] // N
    group_heads = head_count // group_count
    head_width = x_block.shape[1] // head_count
    step_size = step_raw.astype(jnp.float32) * live_rows[None, :]
    decay_sum = jnp.cumsum(-decay_rate[:, None] * step_size, axis=1)
    causal = jnp.arange(row_count)[:, None] >= jnp.arange(row_count)[None, :]
    gap_sum = decay_sum[:, :, None] - decay_sum[:, None, :]
    decay_table = jnp.where(causal[None], jnp.exp(jnp.minimum(gap_sum, 0.0)), 0.0)
    b_split = b_block.astype(jnp.float32).reshape(row_count, group_count, N)
    c_split = c_block.astype(jnp.float32).reshape(row_count, group_count, N)
    scores = jnp.einsum('tgn,ugn->gtu', c_split, b_split, precision=exact_prec)
    mixing = (decay_table.reshape(group_count, group_heads, row_count, row_count) * scores[:, None]
              * step_size.reshape(group_count, group_heads, 1, row_count)).astype(jnp.bfloat16)
    mixing = mixing.reshape(head_count, row_count, row_count)
    x_split = x_block.astype(jnp.float32).reshape(row_count, head_count, head_width)
    within = jnp.einsum('htu,uhp->thp', mixing.astype(jnp.float32), x_split, precision=exact_prec)
    state_split = state_in.reshape(group_count, group_heads, head_width, N)
    carried = jnp.einsum('tgn,gkpn->tgkp', c_split, state_split, precision=exact_prec)
    carried = carried.reshape(row_count, head_count, head_width)
    growth = jnp.exp(decay_sum)
    result = (within + carried * growth.T[:, :, None] + skip_value[None, :, None] * x_split) * live_rows[:, None, None]
    block_end = decay_sum[:, -1]
    to_end = jnp.exp(block_end[:, None] - decay_sum) * step_size
    weighted = (b_split[:, :, None, :] * to_end.reshape(group_count, group_heads, row_count).transpose(2, 0, 1)[..., None]).astype(jnp.bfloat16)
    weighted = weighted.astype(jnp.float32).reshape(row_count, head_count, N)
    fresh_state = jnp.einsum('uhp,uhn->hpn', x_split, weighted, precision=exact_prec)
    new_state = jnp.exp(block_end)[:, None, None] * state_in + fresh_state
    return result.reshape(row_count, head_count * head_width), new_state


def reference(x_rows, b_rows, c_rows, time_step, decay_log, skip_gain, prompt_lengths, block_lists, decode_slot, staying):
    head_count = decay_log.shape[0]
    head_width = x_rows.shape[1] // head_count
    group_count = b_rows.shape[1] // N
    decay_rate = jnp.exp(decay_log)
    x_all = x_rows.reshape(REQS, PER_QUERY_TILES, TILE_HEIGHT, head_count * head_width)
    b_all = b_rows.reshape(REQS, PER_QUERY_TILES, TILE_HEIGHT, group_count * N)
    c_all = c_rows.reshape(REQS, PER_QUERY_TILES, TILE_HEIGHT, group_count * N)
    step_all = time_step.reshape(head_count, REQS, PER_QUERY_TILES, TILE_HEIGHT).transpose(1, 2, 0, 3)
    offsets = jnp.arange(PER_QUERY_TILES)[:, None] * TILE_HEIGHT + jnp.arange(TILE_HEIGHT)[None, :]

    def one_request(request_item):
        x_req, b_req, c_req, step_req, length = request_item
        live_all = (offsets < length).astype(jnp.float32)

        def advance(state_in, block_item):
            x_block, b_block, c_block, step_raw, live_rows = block_item
            result, new_state = block_step(x_block, b_block, c_block, step_raw, live_rows, decay_rate, skip_gain, state_in)
            return new_state, result.astype(jnp.bfloat16)

        start_state = jnp.zeros((head_count, head_width, N), jnp.float32)
        final_state, block_outs = lax.scan(advance, start_state, (x_req, b_req, c_req, step_req, live_all))
        return block_outs, final_state

    block_outs, final_states = lax.map(one_request, (x_all, b_all, c_all, step_all, prompt_lengths))
    flat_rows = block_outs.reshape(REQS * PER_QUERY_TILES, TILE_HEIGHT, head_count * head_width)
    layer_out = jnp.take(flat_rows, block_lists.reshape(-1).astype(jnp.int32), axis=0)
    layer_out = layer_out.reshape(REQS * W * TILE_HEIGHT, head_count * head_width)
    kept_states = final_states * (staying == 1).astype(jnp.float32)[:, None, None, None]
    slot_ids = jnp.arange(DGRP)[:, None, None] * DCAP + jnp.arange(DCAP)[None, :, None]
    moving_map = ((decode_slot[None, None, :] == slot_ids) & (staying == 0)[None, None, :]).astype(jnp.float32)
    split_states = final_states.reshape(REQS, N_HEAD, DEC_REQ, DH, head_width, N)
    decode_all = jnp.einsum('gcr,rkjipn->gjkicpn', moving_map, split_states, precision=exact_prec)
    decode_states = decode_all.reshape(REQS, N_HEAD, DH, DCAP, head_width, N)
    return layer_out, kept_states, decode_states
```

```python
import math

import jax
import jax.numpy as jnp
from jax import lax
from jax.experimental import pallas as pl
from jax.experimental.pallas import tpu as pltpu
from jax.sharding import PartitionSpec as P

N = 128
TILE = 128
W = 6
TAIL = W - 1
DCAP = 12
DEC_REQ = 8
SLOTS = 11
LOG2E = math.log2(math.e)
F32 = jnp.float32
BF16 = jnp.bfloat16


def shifted(block, axis, distance):
    devices = range(lax.axis_size(axis))
    route = [(i - distance, i) for i in devices if i - distance in devices]
    return lax.ppermute(block, axis, route)


def scan_kernel(heads, width, meta, x_ref, b_ref, c_ref, dt_ref, rate_ref, skip_ref, *rest):
    layer_ref, tail_ref, kept_ref, send_ref, state, out = rest[-6:]
    slot = pl.program_id(0)
    length, filled, before, stay = meta[0], meta[1], meta[2], meta[3]

    @pl.when(slot == 0)
    def _():
        state[...] = jnp.zeros_like(state)

    @pl.when(slot < filled)
    def _():
        first = slot * TILE
        row_ids = lax.broadcasted_iota(jnp.int32, (TILE, TILE), 0)
        col_ids = lax.broadcasted_iota(jnp.int32, (TILE, TILE), 1)
        live_cols = lax.broadcasted_iota(jnp.int32, (1, TILE), 1) + first < length
        live_rows = row_ids + first < length
        step = jnp.where(live_cols, dt_ref[...].astype(F32), 0.0)
        upper = jnp.where(row_ids <= col_ids, 1.0, 0.0).astype(BF16)
        total = jnp.dot(step.astype(BF16), upper, preferred_element_type=F32)
        decay = total * rate_ref[...]
        decay_t = decay.T
        end = decay[:, TILE - 1 : TILE]
        to_end = jnp.exp2(end - decay) * step
        b = b_ref[...]
        c = c_ref[...]
        scores = lax.dot_general(c, b, (((1,), (1,)), ((), ())), preferred_element_type=F32)
        scores = jnp.where(row_ids >= col_ids, scores, 0.0)
        b_t = b.astype(F32).T
        left = col_ids < width
        for pair in range(heads // 2):
            cols = pl.ds(pair * TILE, TILE)
            mix, weighted, decay_col = [], [], []
            for h in (2 * pair, 2 * pair + 1):
                column = jnp.broadcast_to(decay_t[:, h : h + 1], (TILE, TILE))
                gap = jnp.minimum(column - decay[h : h + 1, :], 0.0)
                mix.append((jnp.exp2(gap) * scores * step[h : h + 1, :]).astype(BF16))
                weighted.append((b_t * to_end[h : h + 1, :]).astype(BF16))
                decay_col.append(column)
            lhs = jnp.concatenate(
                [jnp.concatenate(mix, axis=1), jnp.concatenate(weighted, axis=1)], axis=0
            )
            x = x_ref[:, cols]
            zero = jnp.zeros_like(x)
            rhs = jnp.concatenate([jnp.where(left, x, zero), jnp.where(left, zero, x)], axis=0)
            both = jnp.dot(lhs, rhs, preferred_element_type=F32)
            held = state[:, cols]
            carried = jnp.dot(c, held.astype(BF16), preferred_element_type=F32)
            growth = jnp.exp2(jnp.where(left, decay_col[0], decay_col[1]))
            result = both[:TILE] + carried * growth + skip_ref[:, cols] * x.astype(F32)
            out[:, cols] = jnp.where(live_rows, result, 0.0).astype(BF16)
            shrink = growth[TILE - 1 : TILE, :]
            state[:, cols] = shrink * held + both[TILE:]

        @pl.when(slot < W - before)
        def _():
            layer_ref[...] = out[...]

        @pl.when(slot >= W - before)
        def _():
            tail_ref[...] = out[...]

        @pl.when(slot == filled - 1)
        def _():
            keep = stay == 1
            for pair in range(heads // 2):
                cols = pl.ds(pair * TILE, TILE)
                final = state[:, cols].T
                kept_ref[cols, :] = jnp.where(keep, final, 0.0)
                send_ref[cols, :] = final.astype(BF16)


def run_chunk(chunk, chunks, meta, x_rows, b_rows, c_rows, time_step, rate, skip, carry):
    head_count = time_step.shape[0]
    heads = head_count // chunks
    columns = x_rows.shape[1]
    width = columns // head_count
    span = columns // chunks
    last = lambda s, m: jnp.minimum(s, m[1] - 1)
    in_specs = [
        pl.BlockSpec((TILE, span), lambda s, m: (last(s, m), chunk)),
        pl.BlockSpec((TILE, N), lambda s, m: (last(s, m), chunk)),
        pl.BlockSpec((TILE, N), lambda s, m: (last(s, m), chunk)),
        pl.BlockSpec((heads, TILE), lambda s, m: (chunk, last(s, m))),
        pl.BlockSpec((heads, TILE), lambda s, m: (chunk, 0)),
        pl.BlockSpec((1, span), lambda s, m: (0, chunk)),
    ]
    aliases = {}
    extra = ()
    if carry is not None:
        extra = carry
        in_specs += [pl.BlockSpec(memory_space=pl.ANY)] * 3
        aliases = {7: 0, 8: 2, 9: 3}
    grid_spec = pltpu.PrefetchScalarGridSpec(
        num_scalar_prefetch=1,
        grid=(SLOTS,),
        in_specs=in_specs,
        out_specs=[
            pl.BlockSpec((TILE, span), lambda s, m: (jnp.minimum(s + m[2], W - 1), chunk)),
            pl.BlockSpec((TILE, span), lambda s, m: (jnp.clip(s - W + m[2], 0, TAIL - 1), 0)),
            pl.BlockSpec((span, N), lambda s, m: (chunk, 0)),
            pl.BlockSpec((span, N), lambda s, m: (chunk, 0)),
        ],
        scratch_shapes=[pltpu.VMEM((N, span), F32), pltpu.VMEM((TILE, span), BF16)],
    )
    layer, tail, kept, send = pl.pallas_call(
        lambda *refs: scan_kernel(heads, width, *refs),
        grid_spec=grid_spec,
        out_shape=[
            jax.ShapeDtypeStruct((W * TILE, columns), BF16),
            jax.ShapeDtypeStruct((TAIL * TILE, span), BF16),
            jax.ShapeDtypeStruct((columns, N), F32),
            jax.ShapeDtypeStruct((columns, N), BF16),
        ],
        input_output_aliases=aliases,
        compiler_params=pltpu.CompilerParams(vmem_limit_bytes=32 * 1024 * 1024),
        cost_estimate=pl.CostEstimate(flops=2 * 10**9, bytes_accessed=8 * 10**6, transcendentals=0),
    )(meta, x_rows, b_rows, c_rows, time_step, rate, skip, *extra)
    return tail, (layer, kept, send)


def place_chunk(chunk, meta, moved, layer):
    span = moved.shape[1]

    def kernel(meta, moved_ref, _, layer_ref, sems):
        copies = []
        for j in range(TAIL):
            rows = pl.ds(j * TILE, TILE)
            copies.append(
                pltpu.make_async_copy(
                    moved_ref.at[rows, :],
                    layer_ref.at[rows, pl.ds(chunk * span, span)],
                    sems.at[j],
                )
            )
        for j in range(TAIL):
            pl.when(j < meta[2])(copies[j].start)
        for j in range(TAIL):
            pl.when(j < meta[2])(copies[j].wait)

    return pl.pallas_call(
        kernel,
        grid_spec=pltpu.PrefetchScalarGridSpec(
            num_scalar_prefetch=1,
            grid=(),
            in_specs=[pl.BlockSpec(memory_space=pl.ANY)] * 2,
            out_specs=pl.BlockSpec(memory_space=pl.ANY),
            scratch_shapes=[pltpu.SemaphoreType.DMA((TAIL,))],
        ),
        out_shape=jax.ShapeDtypeStruct(layer.shape, layer.dtype),
        input_output_aliases={2: 0},
        cost_estimate=pl.CostEstimate(flops=0, bytes_accessed=2 * 10**6, transcendentals=0),
    )(meta, moved, layer)


def place_states(source, arrived):
    _, heads, width, entries = arrived.shape

    def kernel(source, arrived_ref, decode_ref):
        have = source[pl.program_id(0)] >= 0
        decode_ref[:, 0] = jnp.where(have, arrived_ref[0].astype(F32), 0.0)

    return pl.pallas_call(
        kernel,
        grid_spec=pltpu.PrefetchScalarGridSpec(
            num_scalar_prefetch=1,
            grid=(DCAP,),
            in_specs=[
                pl.BlockSpec(
                    (1, heads, width, entries), lambda c, src: (jnp.maximum(src[c], 0), 0, 0, 0)
                )
            ],
            out_specs=pl.BlockSpec((heads, 1, width, entries), lambda c, src: (0, c, 0, 0)),
        ),
        out_shape=jax.ShapeDtypeStruct((heads, DCAP, width, entries), F32),
        cost_estimate=pl.CostEstimate(flops=0, bytes_accessed=5 * 10**6, transcendentals=0),
    )(source, arrived)


def body(
    x_rows,
    b_rows,
    c_rows,
    time_step,
    decay_log,
    skip_gain,
    prompt_lengths,
    block_lists,
    decode_slot,
    staying,
):
    head_count = decay_log.shape[0]
    columns = x_rows.shape[1]
    width = columns // head_count
    chunks = b_rows.shape[1] // N
    req_count = lax.axis_size("req")
    device = lax.axis_index("req")
    filled = (prompt_lengths + TILE - 1) // TILE
    order = jnp.arange(req_count)
    before = jnp.sum(jnp.where(order < device, filled - W, 0))
    mine = order == device
    pick = lambda values: jnp.sum(jnp.where(mine, values, 0))
    meta = jnp.stack([pick(prompt_lengths), pick(filled), before, pick(staying)]).astype(jnp.int32)
    slot_ids = (device // DEC_REQ) * DCAP + jnp.arange(DCAP)
    wanted = (decode_slot[None, :] == slot_ids[:, None]) & (staying == 0)[None, :]
    source = jnp.sum(jnp.where(wanted, order[None, :] + 1, 0), axis=1).astype(jnp.int32) - 1
    rate = jnp.broadcast_to((-LOG2E * jnp.exp(decay_log))[:, None], (head_count, TILE))
    skip = jnp.repeat(skip_gain, width)[None, :]

    carry = None
    moved = []
    for chunk in range(chunks):
        tail, carry = run_chunk(
            chunk, chunks, meta, x_rows, b_rows, c_rows, time_step, rate, skip, carry
        )
        moved.append(shifted(tail, "req", 1))
    layer, kept, send = carry
    pieces = send.reshape(DEC_REQ, head_count // DEC_REQ, width, N)
    groups = req_count // DEC_REQ
    outgoing = jnp.concatenate([pieces] * groups, axis=0) if groups > 1 else pieces
    arrived = lax.all_to_all(outgoing, "req", split_axis=0, concat_axis=0, tiled=True)
    for chunk in range(chunks):
        layer = place_chunk(chunk, meta, moved[chunk], layer)
    decoded = place_states(source, arrived)[None, None]
    return (layer, kept.reshape(1, head_count, width, N), decoded)


def solution(mesh):
    placed = (
        P(("grp", "req"), "head"),
        P(("grp", "req"), "head"),
        P(("grp", "req"), "head"),
        P("head", ("grp", "req")),
        P("head"),
        P("head"),
        P("grp"),
        P("grp", None),
        P("grp"),
        P("grp"),
    )
    return jax.shard_map(
        body,
        mesh=mesh,
        in_specs=placed,
        out_specs=(
            P(("grp", "req"), "head"),
            P(("grp", "req"), "head", None, None),
            P(("grp", "req"), "head", None, None, None, None),
        ),
        check_vma=False,
    )
```

```python
import math

import jax
import jax.numpy as jnp
from jax import lax
from jax.experimental import pallas as pl
from jax.experimental.pallas import tpu as pltpu
from jax.sharding import PartitionSpec as P

N = 128
TILE = 128
W = 6
TAIL = W - 1
DCAP = 12
DEC_REQ = 8
SLOTS = 11
VMEM = 58 * 1024 * 1024
CEILING = 64.0
LOG2E = math.log2(math.e)
F32 = jnp.float32
BF16 = jnp.bfloat16


def shifted(block, axis, distance):
    devices = range(lax.axis_size(axis))
    route = [(i - distance, i) for i in devices if i - distance in devices]
    return lax.ppermute(block, axis, route)


def prepare(prompt_lengths, decode_slot, staying, decay_log, skip_gain):
    req_count = prompt_lengths.shape[0]
    head_count = decay_log.shape[0]

    def kernel(lengths, slots, stays, decay_ref, skip_ref, meta, source, gains):
        device = lax.axis_index("req")
        blocks = lambda r: (lengths[r] + TILE - 1) // TILE
        before = jnp.int32(0)
        for r in range(req_count):
            before += jnp.where(r < device, blocks(r) - W, 0)
        meta[0] = lengths[device]
        meta[1] = blocks(device)
        meta[2] = before
        meta[3] = stays[device]
        first = (device // DEC_REQ) * DCAP
        for c in range(DCAP):
            found = jnp.int32(-1)
            for r in range(req_count):
                found = jnp.where((slots[r] == first + c) & (stays[r] == 0), r, found)
            source[c] = found
        spread = lambda row: jnp.broadcast_to(row, (TILE, head_count)).T
        gains[0] = spread(-LOG2E * jnp.exp(decay_ref[...]))
        gains[1] = spread(skip_ref[...])

    smem = pl.BlockSpec(memory_space=pltpu.SMEM)
    vmem = pl.BlockSpec(memory_space=pltpu.VMEM)
    return pl.pallas_call(
        kernel,
        in_specs=[smem, smem, smem, vmem, vmem],
        out_specs=[smem, smem, vmem],
        out_shape=[
            jax.ShapeDtypeStruct((4,), jnp.int32),
            jax.ShapeDtypeStruct((DCAP,), jnp.int32),
            jax.ShapeDtypeStruct((2, head_count, TILE), F32),
        ],
    )(prompt_lengths, decode_slot, staying, decay_log[None, :], skip_gain[None, :])


def scan_kernel(heads, width, meta, x_ref, b_ref, c_ref, dt_ref, gain_ref, *rest):
    layer_ref, tail_ref, kept_ref, send_ref, state, out = rest[-6:]
    slot = pl.program_id(0)
    length, filled, before, stay = meta[0], meta[1], meta[2], meta[3]

    @pl.when(slot == 0)
    def _():
        state[...] = jnp.zeros_like(state)

    @pl.when(slot < filled)
    def _():
        first = slot * TILE
        row_ids = lax.broadcasted_iota(jnp.int32, (TILE, TILE), 0)
        col_ids = lax.broadcasted_iota(jnp.int32, (TILE, TILE), 1)
        live_cols = lax.broadcasted_iota(jnp.int32, (1, TILE), 1) + first < length
        live_rows = row_ids + first < length
        step = jnp.where(live_cols, dt_ref[...].astype(F32), 0.0)
        upper = jnp.where(row_ids <= col_ids, 1.0, 0.0).astype(BF16)
        total = jnp.dot(step.astype(BF16), upper, preferred_element_type=F32)
        decay = total * gain_ref[0]
        decay_t = decay.T
        end = decay[:, TILE - 1 : TILE]
        to_end = jnp.exp2(end - decay) * step
        offset = decay - jnp.log2(step)
        b = b_ref[...]
        c = c_ref[...]
        scores = lax.dot_general(c, b, (((1,), (1,)), ((), ())), preferred_element_type=F32)
        scores = jnp.where(row_ids >= col_ids, scores, 0.0)
        b_t = b.astype(F32).T
        left = col_ids < width
        for pair in range(heads // 2):
            cols = pl.ds(pair * TILE, TILE)
            mix, weighted, decay_col = [], [], []
            for h in (2 * pair, 2 * pair + 1):
                column = jnp.broadcast_to(decay_t[:, h : h + 1], (TILE, TILE))
                gap = jnp.minimum(column - offset[h : h + 1, :], CEILING)
                mix.append((jnp.exp2(gap) * scores).astype(BF16))
                weighted.append((b_t * to_end[h : h + 1, :]).astype(BF16))
                decay_col.append(column)
            lhs = jnp.concatenate(
                [jnp.concatenate(mix, axis=1), jnp.concatenate(weighted, axis=1)], axis=0
            )
            x = x_ref[:, cols]
            zero = jnp.zeros_like(x)
            rhs = jnp.concatenate([jnp.where(left, x, zero), jnp.where(left, zero, x)], axis=0)
            both = jnp.dot(lhs, rhs, preferred_element_type=F32)
            held = state[:, cols]
            carried = jnp.dot(c, held.astype(BF16), preferred_element_type=F32)
            growth = jnp.exp2(jnp.where(left, decay_col[0], decay_col[1]))
            skip = jnp.where(
                left[:1], gain_ref[1, 2 * pair : 2 * pair + 1, :], gain_ref[1, 2 * pair + 1 : 2 * pair + 2, :]
            )
            result = both[:TILE] + carried * growth + skip * x.astype(F32)
            out[:, cols] = jnp.where(live_rows, result, 0.0).astype(BF16)
            shrink = growth[TILE - 1 : TILE, :]
            state[:, cols] = shrink * held + both[TILE:]

        @pl.when(slot < W - before)
        def _():
            layer_ref[...] = out[...]

        @pl.when(slot >= W - before)
        def _():
            tail_ref[...] = out[...]

        @pl.when(slot == filled - 1)
        def _():
            keep = stay == 1
            for pair in range(heads // 2):
                cols = pl.ds(pair * TILE, TILE)
                final = state[:, cols].T
                kept_ref[cols, :] = jnp.where(keep, final, 0.0)
                send_ref[cols, :] = final.astype(BF16)


def run_chunk(chunk, chunks, meta, x_rows, b_rows, c_rows, time_step, gains, carry):
    head_count = time_step.shape[0]
    heads = head_count // chunks
    columns = x_rows.shape[1]
    width = columns // head_count
    span = columns // chunks
    last = lambda s, m: jnp.minimum(s, m[1] - 1)
    in_specs = [
        pl.BlockSpec((TILE, span), lambda s, m: (last(s, m), chunk)),
        pl.BlockSpec((TILE, N), lambda s, m: (last(s, m), chunk)),
        pl.BlockSpec((TILE, N), lambda s, m: (last(s, m), chunk)),
        pl.BlockSpec((heads, TILE), lambda s, m: (chunk, last(s, m))),
        pl.BlockSpec((2, heads, TILE), lambda s, m: (0, chunk, 0)),
    ]
    aliases = {}
    extra = ()
    if carry is not None:
        extra = carry
        in_specs += [pl.BlockSpec(memory_space=pl.ANY)] * 3
        aliases = {6: 0, 7: 2, 8: 3}
    grid_spec = pltpu.PrefetchScalarGridSpec(
        num_scalar_prefetch=1,
        grid=(SLOTS,),
        in_specs=in_specs,
        out_specs=[
            pl.BlockSpec((TILE, span), lambda s, m: (jnp.minimum(s + m[2], W - 1), chunk)),
            pl.BlockSpec((TILE, span), lambda s, m: (jnp.clip(s - W + m[2], 0, TAIL - 1), 0)),
            pl.BlockSpec((span, N), lambda s, m: (chunk, 0)),
            pl.BlockSpec((span, N), lambda s, m: (chunk, 0)),
        ],
        scratch_shapes=[pltpu.VMEM((N, span), F32), pltpu.VMEM((TILE, span), BF16)],
    )
    layer, tail, kept, send = pl.pallas_call(
        lambda *refs: scan_kernel(heads, width, *refs),
        grid_spec=grid_spec,
        out_shape=[
            jax.ShapeDtypeStruct((W * TILE, columns), BF16),
            jax.ShapeDtypeStruct((TAIL * TILE, span), BF16),
            jax.ShapeDtypeStruct((columns, N), F32),
            jax.ShapeDtypeStruct((columns, N), BF16),
        ],
        input_output_aliases=aliases,
        compiler_params=pltpu.CompilerParams(vmem_limit_bytes=VMEM),
        cost_estimate=pl.CostEstimate(flops=3 * 10**10, bytes_accessed=8 * 10**6, transcendentals=0),
    )(meta, x_rows, b_rows, c_rows, time_step, gains, *extra)
    return tail, (layer, kept, send)


def place_chunk(chunk, meta, moved, layer, after=()):
    span = moved.shape[1]

    def kernel(meta, moved_ref, *rest):
        layer_ref, sems = rest[-2:]
        copies = []
        for j in range(TAIL):
            rows = pl.ds(j * TILE, TILE)
            target = layer_ref.at[rows, pl.ds(chunk * span, span)]
            copies.append(pltpu.make_async_copy(moved_ref.at[rows, :], target, sems.at[j]))
        for j in range(TAIL):
            pl.when(j < meta[2])(copies[j].start)
        for j in range(TAIL):
            pl.when(j < meta[2])(copies[j].wait)

    return pl.pallas_call(
        kernel,
        grid_spec=pltpu.PrefetchScalarGridSpec(
            num_scalar_prefetch=1,
            grid=(),
            in_specs=[pl.BlockSpec(memory_space=pltpu.VMEM)]
            + [pl.BlockSpec(memory_space=pl.ANY)] * (1 + len(after)),
            out_specs=pl.BlockSpec(memory_space=pl.ANY),
            scratch_shapes=[pltpu.SemaphoreType.DMA((TAIL,))],
        ),
        out_shape=jax.ShapeDtypeStruct(layer.shape, layer.dtype),
        input_output_aliases={2: 0},
        compiler_params=pltpu.CompilerParams(vmem_limit_bytes=VMEM // 8),
        cost_estimate=pl.CostEstimate(flops=3 * 10**10, bytes_accessed=2 * 10**6, transcendentals=0),
    )(meta, moved, layer, *after)


def place_states(source, arrived):
    _, heads, width, entries = arrived.shape

    def kernel(source, arrived_ref, decode_ref):
        have = source[pl.program_id(0)] >= 0
        decode_ref[:, 0] = jnp.where(have, arrived_ref[0].astype(F32), 0.0)

    return pl.pallas_call(
        kernel,
        grid_spec=pltpu.PrefetchScalarGridSpec(
            num_scalar_prefetch=1,
            grid=(DCAP,),
            in_specs=[
                pl.BlockSpec(
                    (1, heads, width, entries), lambda c, src: (jnp.maximum(src[c], 0), 0, 0, 0)
                )
            ],
            out_specs=pl.BlockSpec((heads, 1, width, entries), lambda c, src: (0, c, 0, 0)),
        ),
        out_shape=jax.ShapeDtypeStruct((heads, DCAP, width, entries), F32),
        compiler_params=pltpu.CompilerParams(vmem_limit_bytes=VMEM),
        cost_estimate=pl.CostEstimate(flops=0, bytes_accessed=5 * 10**6, transcendentals=0),
    )(source, arrived)


def body(
    x_rows,
    b_rows,
    c_rows,
    time_step,
    decay_log,
    skip_gain,
    prompt_lengths,
    block_lists,
    decode_slot,
    staying,
):
    head_count = decay_log.shape[0]
    columns = x_rows.shape[1]
    width = columns // head_count
    chunks = b_rows.shape[1] // N
    req_count = lax.axis_size("req")
    meta, source, gains = prepare(prompt_lengths, decode_slot, staying, decay_log, skip_gain)
    carry = None
    moved = []
    for chunk in range(chunks):
        if chunk == 2:
            layer = place_chunk(chunk - 2, meta, moved[chunk - 2], carry[0])
            carry = (layer, carry[1], carry[2])
        tail, carry = run_chunk(
            chunk, chunks, meta, x_rows, b_rows, c_rows, time_step, gains, carry
        )
        moved.append(shifted(tail, "req", 1))
    layer, kept, send = carry
    pieces = send.reshape(DEC_REQ, head_count // DEC_REQ, width, N)
    groups = req_count // DEC_REQ
    outgoing = jnp.concatenate([pieces] * groups, axis=0) if groups > 1 else pieces
    arrived = lax.all_to_all(outgoing, "req", split_axis=0, concat_axis=0, tiled=True)
    decoded = place_states(source, arrived)
    for chunk in range(1, chunks):
        after = (decoded,) if chunk == chunks - 1 else ()
        layer = place_chunk(chunk, meta, moved[chunk], layer, after)
    return (layer, kept.reshape(1, head_count, width, N), decoded[None, None])


def solution(mesh):
    placed = (
        P(("grp", "req"), "head"),
        P(("grp", "req"), "head"),
        P(("grp", "req"), "head"),
        P("head", ("grp", "req")),
        P("head"),
        P("head"),
        P("grp"),
        P("grp", None),
        P("grp"),
        P("grp"),
    )
    return jax.shard_map(
        body,
        mesh=mesh,
        in_specs=placed,
        out_specs=(
            P(("grp", "req"), "head"),
            P(("grp", "req"), "head", None, None),
            P(("grp", "req"), "head", None, None, None, None),
        ),
        check_vma=False,
    )
```

```python
import math

import jax
import jax.numpy as jnp
from jax import lax
from jax.experimental import pallas as pl
from jax.experimental.pallas import tpu as pltpu
from jax.sharding import PartitionSpec as P

N = 128
TILE = 128
W = 6
TAIL = W - 1
DCAP = 12
DEC_REQ = 8
SLOTS = 11
VMEM = 58 * 1024 * 1024
CEILING = 64.0
LOG2E = math.log2(math.e)
F32 = jnp.float32
BF16 = jnp.bfloat16


def shifted(block, axis, distance):
    devices = range(lax.axis_size(axis))
    route = [(i - distance, i) for i in devices if i - distance in devices]
    return lax.ppermute(block, axis, route)


def prepare(prompt_lengths, decode_slot, staying, decay_log, skip_gain):
    req_count = prompt_lengths.shape[0]
    head_count = decay_log.shape[0]

    def kernel(lengths, slots, stays, decay_ref, skip_ref, meta, source, gains):
        device = lax.axis_index("req")
        blocks = lambda r: (lengths[r] + TILE - 1) // TILE
        before = jnp.int32(0)
        for r in range(req_count):
            before += jnp.where(r < device, blocks(r) - W, 0)
        meta[0] = lengths[device]
        meta[1] = blocks(device)
        meta[2] = before
        meta[3] = stays[device]
        first = (device // DEC_REQ) * DCAP
        for c in range(DCAP):
            found = jnp.int32(-1)
            for r in range(req_count):
                found = jnp.where((slots[r] == first + c) & (stays[r] == 0), r, found)
            source[c] = found
        spread = lambda row: jnp.broadcast_to(row, (TILE, head_count)).T
        gains[0] = spread(-LOG2E * jnp.exp(decay_ref[...]))
        gains[1] = spread(skip_ref[...])

    smem = pl.BlockSpec(memory_space=pltpu.SMEM)
    vmem = pl.BlockSpec(memory_space=pltpu.VMEM)
    return pl.pallas_call(
        kernel,
        in_specs=[smem, smem, smem, vmem, vmem],
        out_specs=[smem, smem, vmem],
        out_shape=[
            jax.ShapeDtypeStruct((4,), jnp.int32),
            jax.ShapeDtypeStruct((DCAP,), jnp.int32),
            jax.ShapeDtypeStruct((2, head_count, TILE), F32),
        ],
    )(prompt_lengths, decode_slot, staying, decay_log[None, :], skip_gain[None, :])


def scan_kernel(start, groups, heads, width, meta, x_hbm, b_hbm, c_hbm, dt_hbm, gain_ref, *rest):
    outputs = rest[-16 - groups : -13]
    layer_hbm, kept_hbm, send_hbm = outputs[:3]
    tails_hbm = outputs[3:]
    (xs, bs, cs, dts, outs, state, kept, send, rows_d, cols_d, in_sems, out_sems, end_sems) = rest[-13:]
    length, filled, before, stay = meta[0], meta[1], meta[2], meta[3]
    span = xs.shape[2]
    part = span // groups
    per_group = heads // groups
    wide = pl.ds(start * part, span)
    narrow = pl.ds(start * N, groups * N)

    def block(slot):
        return pl.ds(pl.multiple_of(slot * TILE, TILE), TILE)

    def fetches(slot):
        return [
            pltpu.make_async_copy(c_hbm.at[block(slot), narrow], cs.at[slot], in_sems.at[0, slot]),
            pltpu.make_async_copy(b_hbm.at[block(slot), narrow], bs.at[slot], in_sems.at[1, slot]),
            pltpu.make_async_copy(x_hbm.at[block(slot), wide], xs.at[slot], in_sems.at[2, slot]),
        ]

    def to_layer(slot):
        target = layer_hbm.at[block(slot + before), wide]
        return [pltpu.make_async_copy(outs.at[slot], target, out_sems.at[0, slot])]

    def to_tail(slot):
        copies = []
        for g in range(groups):
            target = tails_hbm[g].at[block(slot - W + before)]
            source = outs.at[slot, :, pl.ds(g * part, part)]
            copies.append(pltpu.make_async_copy(source, target, out_sems.at[1 + g, slot]))
        return copies

    steps = pltpu.make_async_copy(
        dt_hbm.at[pl.ds(start * per_group, heads), :], dts, end_sems.at[0]
    )
    steps.start()
    for slot in range(SLOTS):

        @pl.when(slot < filled)
        def _():
            for copy in fetches(slot):
                copy.start()

    state[...] = jnp.zeros_like(state)
    row_ids = lax.broadcasted_iota(jnp.int32, (TILE, TILE), 0)
    col_ids = lax.broadcasted_iota(jnp.int32, (TILE, TILE), 1)
    left = col_ids < width
    upper = jnp.where(row_ids <= col_ids, 1.0, 0.0).astype(BF16)
    rate = gain_ref[0, start * per_group : start * per_group + heads, :]
    steps.wait()
    for slot in range(SLOTS):
        live = lax.broadcasted_iota(jnp.int32, (1, TILE), 1) + slot * TILE < length
        step = jnp.where(live, dts[:, slot * TILE : (slot + 1) * TILE].astype(F32), 0.0)
        total = jnp.dot(step.astype(BF16), upper, preferred_element_type=F32)
        decay = total * rate
        rows_d[slot, 0] = decay - jnp.log2(step)
        rows_d[slot, 1] = jnp.exp2(decay[:, TILE - 1 : TILE] - decay) * step
        cols_d[slot] = decay.T

    def advance(slot, _):
        for copy in fetches(slot):
            copy.wait()
        live_rows = row_ids + slot * TILE < length
        shared = []
        for g in range(groups):
            b = bs[slot, :, g * N : (g + 1) * N]
            c = cs[slot, :, g * N : (g + 1) * N]
            scores = lax.dot_general(c, b, (((1,), (1,)), ((), ())), preferred_element_type=F32)
            scores = jnp.where(row_ids >= col_ids, scores, 0.0)
            shared.append((c, scores, b.astype(F32).T))
        offset = rows_d[slot, 0]
        to_end = rows_d[slot, 1]
        decay_t = cols_d[slot]
        for pair in range(heads // 2):
            cols = pl.ds(pair * TILE, TILE)
            c, scores, b_t = shared[2 * pair // per_group]
            mix, weighted, decay_col = [], [], []
            for h in (2 * pair, 2 * pair + 1):
                column = jnp.broadcast_to(decay_t[:, h : h + 1], (TILE, TILE))
                gap = jnp.minimum(column - offset[h : h + 1, :], CEILING)
                mix.append((jnp.exp2(gap) * scores).astype(BF16))
                weighted.append((b_t * to_end[h : h + 1, :]).astype(BF16))
                decay_col.append(column)
            lhs = jnp.concatenate(
                [jnp.concatenate(mix, axis=1), jnp.concatenate(weighted, axis=1)], axis=0
            )
            x = xs[slot, :, cols]
            zero = jnp.zeros_like(x)
            rhs = jnp.concatenate([jnp.where(left, x, zero), jnp.where(left, zero, x)], axis=0)
            both = jnp.dot(lhs, rhs, preferred_element_type=F32)
            held = state[:, cols]
            carried = jnp.dot(c, held.astype(BF16), preferred_element_type=F32)
            growth = jnp.exp2(jnp.where(left, decay_col[0], decay_col[1]))
            first = start * per_group + 2 * pair
            skip = jnp.where(
                left[:1], gain_ref[1, first : first + 1, :], gain_ref[1, first + 1 : first + 2, :]
            )
            result = both[:TILE] + carried * growth + skip * x.astype(F32)
            outs[slot, :, cols] = jnp.where(live_rows, result, 0.0).astype(BF16)
            shrink = growth[TILE - 1 : TILE, :]
            state[:, cols] = shrink * held + both[TILE:]

        @pl.when(slot < W - before)
        def _():
            for copy in to_layer(slot):
                copy.start()

        @pl.when(slot >= W - before)
        def _():
            for copy in to_tail(slot):
                copy.start()

        return 0

    lax.fori_loop(0, filled, advance, 0)
    keep = stay == 1
    for pair in range(heads // 2):
        cols = pl.ds(pair * TILE, TILE)
        final = state[:, cols].T
        kept[cols, :] = jnp.where(keep, final, 0.0)
        send[cols, :] = final.astype(BF16)
    last = [
        pltpu.make_async_copy(kept, kept_hbm.at[wide], end_sems.at[1]),
        pltpu.make_async_copy(send, send_hbm.at[wide], end_sems.at[2]),
    ]
    for copy in last:
        copy.start()

    def drain(slot, _):
        @pl.when(slot < W - before)
        def _():
            for copy in to_layer(slot):
                copy.wait()

        @pl.when(slot >= W - before)
        def _():
            for copy in to_tail(slot):
                copy.wait()

        return 0

    lax.fori_loop(0, filled, drain, 0)
    for copy in last:
        copy.wait()


def run_groups(start, groups, total, meta, x_rows, b_rows, c_rows, time_step, gains, carry):
    head_count = time_step.shape[0]
    heads = head_count // total * groups
    columns = x_rows.shape[1]
    width = columns // head_count
    part = columns // total
    span = part * groups
    whole = pl.BlockSpec(memory_space=pl.ANY)
    in_specs = [whole] * 4 + [pl.BlockSpec(memory_space=pltpu.VMEM)]
    aliases = {}
    extra = ()
    if carry is not None:
        extra = carry
        in_specs += [whole] * 3
        aliases = {6: 0, 7: 1, 8: 2}
    grid_spec = pltpu.PrefetchScalarGridSpec(
        num_scalar_prefetch=1,
        grid=(),
        in_specs=in_specs,
        out_specs=[whole] * (3 + groups),
        scratch_shapes=[
            pltpu.VMEM((SLOTS, TILE, span), BF16),
            pltpu.VMEM((SLOTS, TILE, groups * N), BF16),
            pltpu.VMEM((SLOTS, TILE, groups * N), BF16),
            pltpu.VMEM((heads, SLOTS * TILE), BF16),
            pltpu.VMEM((SLOTS, TILE, span), BF16),
            pltpu.VMEM((N, span), F32),
            pltpu.VMEM((span, N), F32),
            pltpu.VMEM((span, N), BF16),
            pltpu.VMEM((SLOTS, 2, heads, TILE), F32),
            pltpu.VMEM((SLOTS, TILE, heads), F32),
            pltpu.SemaphoreType.DMA((3, SLOTS)),
            pltpu.SemaphoreType.DMA((1 + groups, SLOTS)),
            pltpu.SemaphoreType.DMA((3,)),
        ],
    )
    layer, kept, send, *tails = pl.pallas_call(
        lambda *refs: scan_kernel(start, groups, heads, width, *refs),
        grid_spec=grid_spec,
        out_shape=[
            jax.ShapeDtypeStruct((W * TILE, columns), BF16),
            jax.ShapeDtypeStruct((columns, N), F32),
            jax.ShapeDtypeStruct((columns, N), BF16),
        ]
        + [jax.ShapeDtypeStruct((TAIL * TILE, part), BF16)] * groups,
        input_output_aliases=aliases,
        compiler_params=pltpu.CompilerParams(vmem_limit_bytes=VMEM),
        cost_estimate=pl.CostEstimate(flops=3 * 10**10, bytes_accessed=8 * 10**6, transcendentals=0),
    )(meta, x_rows, b_rows, c_rows, time_step, gains, *extra)
    return tails, (layer, kept, send)


def place_chunk(chunk, meta, moved, layer, after=()):
    span = moved.shape[1]

    def kernel(meta, moved_ref, *rest):
        layer_ref, sems = rest[-2:]
        copies = []
        for j in range(TAIL):
            rows = pl.ds(j * TILE, TILE)
            target = layer_ref.at[rows, pl.ds(chunk * span, span)]
            copies.append(pltpu.make_async_copy(moved_ref.at[rows, :], target, sems.at[j]))
        for j in range(TAIL):
            pl.when(j < meta[2])(copies[j].start)
        for j in range(TAIL):
            pl.when(j < meta[2])(copies[j].wait)

    return pl.pallas_call(
        kernel,
        grid_spec=pltpu.PrefetchScalarGridSpec(
            num_scalar_prefetch=1,
            grid=(),
            in_specs=[pl.BlockSpec(memory_space=pltpu.VMEM)]
            + [pl.BlockSpec(memory_space=pl.ANY)] * (1 + len(after)),
            out_specs=pl.BlockSpec(memory_space=pl.ANY),
            scratch_shapes=[pltpu.SemaphoreType.DMA((TAIL,))],
        ),
        out_shape=jax.ShapeDtypeStruct(layer.shape, layer.dtype),
        input_output_aliases={2: 0},
        compiler_params=pltpu.CompilerParams(vmem_limit_bytes=VMEM // 8),
        cost_estimate=pl.CostEstimate(flops=3 * 10**10, bytes_accessed=2 * 10**6, transcendentals=0),
    )(meta, moved, layer, *after)


def place_states(source, arrived):
    _, heads, width, entries = arrived.shape

    def kernel(source, arrived_ref, decode_ref):
        have = source[pl.program_id(0)] >= 0
        decode_ref[:, 0] = jnp.where(have, arrived_ref[0].astype(F32), 0.0)

    return pl.pallas_call(
        kernel,
        grid_spec=pltpu.PrefetchScalarGridSpec(
            num_scalar_prefetch=1,
            grid=(DCAP,),
            in_specs=[
                pl.BlockSpec(
                    (1, heads, width, entries), lambda c, src: (jnp.maximum(src[c], 0), 0, 0, 0)
                )
            ],
            out_specs=pl.BlockSpec((heads, 1, width, entries), lambda c, src: (0, c, 0, 0)),
        ),
        out_shape=jax.ShapeDtypeStruct((heads, DCAP, width, entries), F32),
        compiler_params=pltpu.CompilerParams(vmem_limit_bytes=VMEM),
        cost_estimate=pl.CostEstimate(flops=0, bytes_accessed=5 * 10**6, transcendentals=0),
    )(source, arrived)


def body(
    x_rows,
    b_rows,
    c_rows,
    time_step,
    decay_log,
    skip_gain,
    prompt_lengths,
    block_lists,
    decode_slot,
    staying,
):
    head_count = decay_log.shape[0]
    columns = x_rows.shape[1]
    width = columns // head_count
    chunks = b_rows.shape[1] // N
    req_count = lax.axis_size("req")
    meta, source, gains = prepare(prompt_lengths, decode_slot, staying, decay_log, skip_gain)
    moved = []
    carry = None
    for start, groups in ((0, 1), (1, chunks - 1)):
        tails, carry = run_groups(
            start, groups, chunks, meta, x_rows, b_rows, c_rows, time_step, gains, carry
        )
        moved += [shifted(tail, "req", 1) for tail in tails]
    layer, kept, send = carry
    pieces = send.reshape(DEC_REQ, head_count // DEC_REQ, width, N)
    groups = req_count // DEC_REQ
    outgoing = jnp.concatenate([pieces] * groups, axis=0) if groups > 1 else pieces
    arrived = lax.all_to_all(outgoing, "req", split_axis=0, concat_axis=0, tiled=True)
    decoded = place_states(source, arrived)
    for chunk in range(chunks):
        after = (decoded,) if chunk == 1 else ()
        layer = place_chunk(chunk, meta, moved[chunk], layer, after)
    return (layer, kept.reshape(1, head_count, width, N), decoded[None, None])


def solution(mesh):
    placed = (
        P(("grp", "req"), "head"),
        P(("grp", "req"), "head"),
        P(("grp", "req"), "head"),
        P("head", ("grp", "req")),
        P("head"),
        P("head"),
        P("grp"),
        P("grp", None),
        P("grp"),
        P("grp"),
    )
    return jax.shard_map(
        body,
        mesh=mesh,
        in_specs=placed,
        out_specs=(
            P(("grp", "req"), "head"),
            P(("grp", "req"), "head", None, None),
            P(("grp", "req"), "head", None, None, None, None),
        ),
        check_vma=False,
    )
```

```python
import math

import jax
import jax.numpy as jnp
from jax import lax
from jax.experimental import pallas as pl
from jax.experimental.pallas import tpu as pltpu
from jax.sharding import PartitionSpec as P

N = 128
TILE = 128
W = 6
TAIL = W - 1
DCAP = 12
DEC_REQ = 8
SLOTS = 11
VMEM = 58 * 1024 * 1024
CEILING = 64.0
LOG2E = math.log2(math.e)
F32 = jnp.float32
BF16 = jnp.bfloat16


def shifted(block, axis, distance):
    devices = range(lax.axis_size(axis))
    route = [(i - distance, i) for i in devices if i - distance in devices]
    return lax.ppermute(block, axis, route)


def prepare(prompt_lengths, decode_slot, staying, decay_log, skip_gain):
    req_count = prompt_lengths.shape[0]
    head_count = decay_log.shape[0]

    def kernel(lengths, slots, stays, decay_ref, skip_ref, meta, source, gains):
        device = lax.axis_index("req")
        blocks = lambda r: (lengths[r] + TILE - 1) // TILE
        before = jnp.int32(0)
        for r in range(req_count):
            before += jnp.where(r < device, blocks(r) - W, 0)
        meta[0] = lengths[device]
        meta[1] = blocks(device)
        meta[2] = before
        meta[3] = stays[device]
        first = (device // DEC_REQ) * DCAP
        for c in range(DCAP):
            found = jnp.int32(-1)
            for r in range(req_count):
                found = jnp.where((slots[r] == first + c) & (stays[r] == 0), r, found)
            source[c] = found
        spread = lambda row: jnp.broadcast_to(row, (TILE, head_count)).T
        gains[0] = spread(-LOG2E * jnp.exp(decay_ref[...]))
        gains[1] = spread(skip_ref[...])

    smem = pl.BlockSpec(memory_space=pltpu.SMEM)
    vmem = pl.BlockSpec(memory_space=pltpu.VMEM)
    return pl.pallas_call(
        kernel,
        in_specs=[smem, smem, smem, vmem, vmem],
        out_specs=[smem, smem, vmem],
        out_shape=[
            jax.ShapeDtypeStruct((4,), jnp.int32),
            jax.ShapeDtypeStruct((DCAP,), jnp.int32),
            jax.ShapeDtypeStruct((2, head_count, TILE), F32),
        ],
    )(prompt_lengths, decode_slot, staying, decay_log[None, :], skip_gain[None, :])


def scan_kernel(start, groups, heads, width, meta, x_hbm, b_hbm, c_hbm, dt_hbm, gain_ref, *rest):
    outputs = rest[-13 - groups : -11]
    layer_hbm, state_hbm = outputs[:2]
    tails_hbm = outputs[2:]
    (xs, bs, cs, dts, outs, state, rows_d, cols_d, in_sems, out_sems, end_sems) = rest[-11:]
    length, filled, before = meta[0], meta[1], meta[2]
    span = xs.shape[2]
    part = span // groups
    per_group = heads // groups
    wide = pl.ds(start * part, span)
    narrow = pl.ds(start * N, groups * N)

    def block(slot):
        return pl.ds(pl.multiple_of(slot * TILE, TILE), TILE)

    def fetches(slot):
        return [
            pltpu.make_async_copy(c_hbm.at[block(slot), narrow], cs.at[slot], in_sems.at[0, slot]),
            pltpu.make_async_copy(b_hbm.at[block(slot), narrow], bs.at[slot], in_sems.at[1, slot]),
            pltpu.make_async_copy(x_hbm.at[block(slot), wide], xs.at[slot], in_sems.at[2, slot]),
        ]

    def to_layer(slot):
        target = layer_hbm.at[block(slot + before), wide]
        return [pltpu.make_async_copy(outs.at[slot], target, out_sems.at[0, slot])]

    def to_tail(slot):
        copies = []
        for g in range(groups):
            target = tails_hbm[g].at[block(slot - W + before)]
            source = outs.at[slot, :, pl.ds(g * part, part)]
            copies.append(pltpu.make_async_copy(source, target, out_sems.at[1 + g, slot]))
        return copies

    steps = pltpu.make_async_copy(
        dt_hbm.at[pl.ds(start * per_group, heads), :], dts, end_sems.at[0]
    )
    steps.start()
    for slot in range(SLOTS):

        @pl.when(slot < filled)
        def _():
            for copy in fetches(slot):
                copy.start()

    state[...] = jnp.zeros_like(state)
    row_ids = lax.broadcasted_iota(jnp.int32, (TILE, TILE), 0)
    col_ids = lax.broadcasted_iota(jnp.int32, (TILE, TILE), 1)
    left = col_ids < width
    upper = jnp.where(row_ids <= col_ids, 1.0, 0.0).astype(BF16)
    rate = gain_ref[0, start * per_group : start * per_group + heads, :]
    steps.wait()

    def sums(slot):
        live = lax.broadcasted_iota(jnp.int32, (1, TILE), 1) + slot * TILE < length
        step = jnp.where(live, dts[:, block(slot)].astype(F32), 0.0)
        total = jnp.dot(step.astype(BF16), upper, preferred_element_type=F32)
        decay = total * rate
        rows_d[slot, 0] = decay - jnp.log2(step)
        rows_d[slot, 1] = jnp.exp2(decay[:, TILE - 1 : TILE] - decay) * step
        cols_d[slot] = decay.T

    sums(0)

    def advance(slot, _):
        for copy in fetches(slot):
            copy.wait()
        live_rows = row_ids + slot * TILE < length
        shared = []
        for g in range(groups):
            b = bs[slot, :, g * N : (g + 1) * N]
            c = cs[slot, :, g * N : (g + 1) * N]
            scores = lax.dot_general(c, b, (((1,), (1,)), ((), ())), preferred_element_type=F32)
            scores = jnp.where(row_ids >= col_ids, scores, 0.0)
            shared.append((c, scores, b.astype(F32).T))
        offset = rows_d[slot, 0]
        to_end = rows_d[slot, 1]
        decay_t = cols_d[slot]
        for pair in range(heads // 2):
            cols = pl.ds(pair * TILE, TILE)
            c, scores, b_t = shared[2 * pair // per_group]
            mix, weighted, decay_col = [], [], []
            for h in (2 * pair, 2 * pair + 1):
                column = jnp.broadcast_to(decay_t[:, h : h + 1], (TILE, TILE))
                gap = jnp.minimum(column - offset[h : h + 1, :], CEILING)
                mix.append((jnp.exp2(gap) * scores).astype(BF16))
                weighted.append((b_t * to_end[h : h + 1, :]).astype(BF16))
                decay_col.append(column)
            lhs = jnp.concatenate(
                [jnp.concatenate(mix, axis=1), jnp.concatenate(weighted, axis=1)], axis=0
            )
            x = xs[slot, :, cols]
            zero = jnp.zeros_like(x)
            rhs = jnp.concatenate([jnp.where(left, x, zero), jnp.where(left, zero, x)], axis=0)
            both = jnp.dot(lhs, rhs, preferred_element_type=F32)
            held = state[:, cols]
            carried = jnp.dot(c, held.astype(BF16), preferred_element_type=F32)
            growth = jnp.exp2(jnp.where(left, decay_col[0], decay_col[1]))
            first = start * per_group + 2 * pair
            skip = jnp.where(
                left[:1], gain_ref[1, first : first + 1, :], gain_ref[1, first + 1 : first + 2, :]
            )
            result = both[:TILE] + carried * growth + skip * x.astype(F32)
            outs[slot, :, cols] = jnp.where(live_rows, result, 0.0).astype(BF16)
            shrink = growth[TILE - 1 : TILE, :]
            state[:, cols] = shrink * held + both[TILE:]
        sums(jnp.minimum(slot + 1, SLOTS - 1))

        @pl.when(slot < W - before)
        def _():
            for copy in to_layer(slot):
                copy.start()

        @pl.when(slot >= W - before)
        def _():
            for copy in to_tail(slot):
                copy.start()

        return 0

    lax.fori_loop(0, filled, advance, 0)
    last = pltpu.make_async_copy(state, state_hbm.at[:, wide], end_sems.at[1])
    last.start()

    def drain(slot, _):
        @pl.when(slot < W - before)
        def _():
            for copy in to_layer(slot):
                copy.wait()

        @pl.when(slot >= W - before)
        def _():
            for copy in to_tail(slot):
                copy.wait()

        return 0

    lax.fori_loop(0, filled, drain, 0)
    last.wait()


def run_groups(start, groups, total, meta, x_rows, b_rows, c_rows, time_step, gains, carry):
    head_count = time_step.shape[0]
    heads = head_count // total * groups
    columns = x_rows.shape[1]
    width = columns // head_count
    part = columns // total
    span = part * groups
    whole = pl.BlockSpec(memory_space=pl.ANY)
    in_specs = [whole] * 4 + [pl.BlockSpec(memory_space=pltpu.VMEM)]
    aliases = {}
    extra = ()
    if carry is not None:
        extra = carry
        in_specs += [whole] * 2
        aliases = {6: 0, 7: 1}
    grid_spec = pltpu.PrefetchScalarGridSpec(
        num_scalar_prefetch=1,
        grid=(),
        in_specs=in_specs,
        out_specs=[whole] * (2 + groups),
        scratch_shapes=[
            pltpu.VMEM((SLOTS, TILE, span), BF16),
            pltpu.VMEM((SLOTS, TILE, groups * N), BF16),
            pltpu.VMEM((SLOTS, TILE, groups * N), BF16),
            pltpu.VMEM((heads, SLOTS * TILE), BF16),
            pltpu.VMEM((SLOTS, TILE, span), BF16),
            pltpu.VMEM((N, span), F32),
            pltpu.VMEM((SLOTS, 2, heads, TILE), F32),
            pltpu.VMEM((SLOTS, TILE, heads), F32),
            pltpu.SemaphoreType.DMA((3, SLOTS)),
            pltpu.SemaphoreType.DMA((1 + groups, SLOTS)),
            pltpu.SemaphoreType.DMA((2,)),
        ],
    )
    layer, state, *tails = pl.pallas_call(
        lambda *refs: scan_kernel(start, groups, heads, width, *refs),
        grid_spec=grid_spec,
        out_shape=[
            jax.ShapeDtypeStruct((W * TILE, columns), BF16),
            jax.ShapeDtypeStruct((N, columns), F32),
        ]
        + [jax.ShapeDtypeStruct((TAIL * TILE, part), BF16)] * groups,
        input_output_aliases=aliases,
        compiler_params=pltpu.CompilerParams(vmem_limit_bytes=VMEM),
        cost_estimate=pl.CostEstimate(flops=3 * 10**10, bytes_accessed=8 * 10**6, transcendentals=0),
    )(meta, x_rows, b_rows, c_rows, time_step, gains, *extra)
    return tails, (layer, state)


def finish(meta, state, token):
    columns = state.shape[1]
    span = columns // 4

    def kernel(meta, state_ref, token, kept_ref, send_ref):
        for part in range(span // TILE):
            cols = pl.ds(part * TILE, TILE)
            final = state_ref[:, cols].T
            kept_ref[cols, :] = jnp.where(meta[3] == 1, final, 0.0)
            send_ref[cols, :] = final.astype(BF16)

    return pl.pallas_call(
        kernel,
        grid_spec=pltpu.PrefetchScalarGridSpec(
            num_scalar_prefetch=1,
            grid=(columns // span,),
            in_specs=[
                pl.BlockSpec((N, span), lambda i, m: (0, i)),
                pl.BlockSpec(memory_space=pltpu.SMEM),
            ],
            out_specs=[pl.BlockSpec((span, N), lambda i, m: (i, 0))] * 2,
        ),
        out_shape=[
            jax.ShapeDtypeStruct((columns, N), F32),
            jax.ShapeDtypeStruct((columns, N), BF16),
        ],
        compiler_params=pltpu.CompilerParams(vmem_limit_bytes=VMEM),
        cost_estimate=pl.CostEstimate(flops=3 * 10**10, bytes_accessed=5 * 10**6, transcendentals=0),
    )(meta, state, token)


def place_chunk(chunk, meta, moved, layer, after=()):
    span = moved.shape[1]

    def kernel(meta, moved_ref, *rest):
        layer_ref, token, sems = rest[-3:]
        token[0] = 0
        copies = []
        for j in range(TAIL):
            rows = pl.ds(j * TILE, TILE)
            target = layer_ref.at[rows, pl.ds(chunk * span, span)]
            copies.append(pltpu.make_async_copy(moved_ref.at[rows, :], target, sems.at[j]))
        for j in range(TAIL):
            pl.when(j < meta[2])(copies[j].start)
        for j in range(TAIL):
            pl.when(j < meta[2])(copies[j].wait)

    return pl.pallas_call(
        kernel,
        grid_spec=pltpu.PrefetchScalarGridSpec(
            num_scalar_prefetch=1,
            grid=(),
            in_specs=[pl.BlockSpec(memory_space=pltpu.VMEM)]
            + [pl.BlockSpec(memory_space=pl.ANY)]
            + [pl.BlockSpec(memory_space=pltpu.SMEM)] * len(after),
            out_specs=[pl.BlockSpec(memory_space=pl.ANY), pl.BlockSpec(memory_space=pltpu.SMEM)],
            scratch_shapes=[pltpu.SemaphoreType.DMA((TAIL,))],
        ),
        out_shape=[
            jax.ShapeDtypeStruct(layer.shape, layer.dtype),
            jax.ShapeDtypeStruct((1,), jnp.int32),
        ],
        input_output_aliases={2: 0},
        compiler_params=pltpu.CompilerParams(vmem_limit_bytes=VMEM // 8),
        cost_estimate=pl.CostEstimate(flops=3 * 10**10, bytes_accessed=2 * 10**6, transcendentals=0),
    )(meta, moved, layer, *after)


def place_states(source, arrived):
    _, heads, width, entries = arrived.shape

    def kernel(source, arrived_ref, decode_hbm, token, held, sems):
        copies = []
        for c in range(DCAP):
            request = source[c]
            value = arrived_ref[jnp.maximum(request, 0)].astype(F32)
            held[c] = jnp.where(request >= 0, value, 0.0)
            copies.append(pltpu.make_async_copy(held.at[c], decode_hbm.at[:, c], sems.at[c]))
            copies[c].start()
        token[0] = 0
        for copy in copies:
            copy.wait()

    return pl.pallas_call(
        kernel,
        grid_spec=pltpu.PrefetchScalarGridSpec(
            num_scalar_prefetch=1,
            grid=(),
            in_specs=[pl.BlockSpec(memory_space=pltpu.VMEM)],
            out_specs=[pl.BlockSpec(memory_space=pl.ANY), pl.BlockSpec(memory_space=pltpu.SMEM)],
            scratch_shapes=[
                pltpu.VMEM((DCAP, heads, width, entries), F32),
                pltpu.SemaphoreType.DMA((DCAP,)),
            ],
        ),
        out_shape=[
            jax.ShapeDtypeStruct((heads, DCAP, width, entries), F32),
            jax.ShapeDtypeStruct((1,), jnp.int32),
        ],
        compiler_params=pltpu.CompilerParams(vmem_limit_bytes=VMEM),
        cost_estimate=pl.CostEstimate(flops=0, bytes_accessed=5 * 10**6, transcendentals=0),
    )(source, arrived)


def body(
    x_rows,
    b_rows,
    c_rows,
    time_step,
    decay_log,
    skip_gain,
    prompt_lengths,
    block_lists,
    decode_slot,
    staying,
):
    head_count = decay_log.shape[0]
    columns = x_rows.shape[1]
    width = columns // head_count
    chunks = b_rows.shape[1] // N
    req_count = lax.axis_size("req")
    meta, source, gains = prepare(prompt_lengths, decode_slot, staying, decay_log, skip_gain)
    moved = []
    carry = None
    for start, groups in ((0, 1), (1, chunks - 1)):
        tails, carry = run_groups(
            start, groups, chunks, meta, x_rows, b_rows, c_rows, time_step, gains, carry
        )
        moved += [shifted(tail, "req", 1) for tail in tails]
    layer, state = carry
    token = None
    for turn, chunk in enumerate((0, *range(chunks - 1, 0, -1))):
        if turn == 1:
            kept, send = finish(meta, state, token)
            pieces = send.reshape(DEC_REQ, head_count // DEC_REQ, width, N)
            groups = req_count // DEC_REQ
            outgoing = jnp.concatenate([pieces] * groups, axis=0) if groups > 1 else pieces
            arrived = lax.all_to_all(outgoing, "req", split_axis=0, concat_axis=0, tiled=True)
        if turn == chunks - 1:
            decoded, token = place_states(source, arrived)
        after = (token,) if turn == chunks - 1 else ()
        layer, token = place_chunk(chunk, meta, moved[chunk], layer, after)
    return (layer, kept.reshape(1, head_count, width, N), decoded[None, None])


def solution(mesh):
    placed = (
        P(("grp", "req"), "head"),
        P(("grp", "req"), "head"),
        P(("grp", "req"), "head"),
        P("head", ("grp", "req")),
        P("head"),
        P("head"),
        P("grp"),
        P("grp", None),
        P("grp"),
        P("grp"),
    )
    return jax.shard_map(
        body,
        mesh=mesh,
        in_specs=placed,
        out_specs=(
            P(("grp", "req"), "head"),
            P(("grp", "req"), "head", None, None),
            P(("grp", "req"), "head", None, None, None, None),
        ),
        check_vma=False,
    )
```

```python
import math

import jax
import jax.numpy as jnp
from jax import lax
from jax.experimental import pallas as pl
from jax.experimental.pallas import tpu as pltpu
from jax.sharding import PartitionSpec as P

N = 128
TILE = 128
W = 6
TAIL = W - 1
DCAP = 12
DEC_REQ = 8
SLOTS = 11
VMEM = 58 * 1024 * 1024
CEILING = 64.0
LOG2E = math.log2(math.e)
F32 = jnp.float32
BF16 = jnp.bfloat16


def shifted(block, axis, distance):
    devices = range(lax.axis_size(axis))
    route = [(i - distance, i) for i in devices if i - distance in devices]
    return lax.ppermute(block, axis, route)


def prepare(prompt_lengths, decode_slot, staying, decay_log, skip_gain):
    req_count = prompt_lengths.shape[0]
    head_count = decay_log.shape[0]

    def kernel(lengths, slots, stays, decay_ref, skip_ref, meta, source, gains):
        device = lax.axis_index("req")
        blocks = lambda r: (lengths[r] + TILE - 1) // TILE
        before = jnp.int32(0)
        for r in range(req_count):
            before += jnp.where(r < device, blocks(r) - W, 0)
        meta[0] = lengths[device]
        meta[1] = blocks(device)
        meta[2] = before
        meta[3] = stays[device]
        first = (device // DEC_REQ) * DCAP
        for c in range(DCAP):
            found = jnp.int32(-1)
            for r in range(req_count):
                found = jnp.where((slots[r] == first + c) & (stays[r] == 0), r, found)
            source[c] = found
        spread = lambda row: jnp.broadcast_to(row, (TILE, head_count)).T
        gains[0] = spread(-LOG2E * jnp.exp(decay_ref[...]))
        gains[1] = spread(skip_ref[...])

    smem = pl.BlockSpec(memory_space=pltpu.SMEM)
    vmem = pl.BlockSpec(memory_space=pltpu.VMEM)
    return pl.pallas_call(
        kernel,
        in_specs=[smem, smem, smem, vmem, vmem],
        out_specs=[smem, smem, vmem],
        out_shape=[
            jax.ShapeDtypeStruct((4,), jnp.int32),
            jax.ShapeDtypeStruct((DCAP,), jnp.int32),
            jax.ShapeDtypeStruct((2, head_count, TILE), F32),
        ],
    )(prompt_lengths, decode_slot, staying, decay_log[None, :], skip_gain[None, :])


def scan_kernel(start, groups, heads, width, meta, x_hbm, b_hbm, c_hbm, dt_hbm, gain_ref, *rest):
    outputs = rest[-13 - groups : -11]
    layer_hbm, state_hbm = outputs[:2]
    tails_hbm = outputs[2:]
    (xs, bs, cs, dts, outs, state, rows_d, cols_d, in_sems, out_sems, end_sems) = rest[-11:]
    length, filled, before = meta[0], meta[1], meta[2]
    span = xs.shape[2]
    part = span // groups
    per_group = heads // groups
    wide = pl.ds(start * part, span)
    narrow = pl.ds(start * N, groups * N)

    def block(slot):
        return pl.ds(pl.multiple_of(slot * TILE, TILE), TILE)

    def fetches(slot):
        return [
            pltpu.make_async_copy(c_hbm.at[block(slot), narrow], cs.at[slot], in_sems.at[0, slot]),
            pltpu.make_async_copy(b_hbm.at[block(slot), narrow], bs.at[slot], in_sems.at[1, slot]),
            pltpu.make_async_copy(x_hbm.at[block(slot), wide], xs.at[slot], in_sems.at[2, slot]),
        ]

    def to_layer(slot):
        target = layer_hbm.at[block(slot + before), wide]
        return [pltpu.make_async_copy(outs.at[slot], target, out_sems.at[0, slot])]

    def to_tail(slot):
        copies = []
        for g in range(groups):
            target = tails_hbm[g].at[block(slot - W + before)]
            source = outs.at[slot, :, pl.ds(g * part, part)]
            copies.append(pltpu.make_async_copy(source, target, out_sems.at[1 + g, slot]))
        return copies

    steps = pltpu.make_async_copy(
        dt_hbm.at[pl.ds(start * per_group, heads), :], dts, end_sems.at[0]
    )
    steps.start()
    for slot in range(SLOTS):

        @pl.when(slot < filled)
        def _():
            for copy in fetches(slot):
                copy.start()

    state[...] = jnp.zeros_like(state)
    row_ids = lax.broadcasted_iota(jnp.int32, (TILE, TILE), 0)
    col_ids = lax.broadcasted_iota(jnp.int32, (TILE, TILE), 1)
    left = col_ids < width
    upper = jnp.where(row_ids <= col_ids, 1.0, 0.0).astype(BF16)
    rate = gain_ref[0, start * per_group : start * per_group + heads, :]
    steps.wait()

    def sums(slot):
        live = lax.broadcasted_iota(jnp.int32, (1, TILE), 1) + slot * TILE < length
        step = jnp.where(live, dts[:, block(slot)].astype(F32), 0.0)
        total = jnp.dot(step.astype(BF16), upper, preferred_element_type=F32)
        decay = total * rate
        rows_d[slot, 0] = decay - jnp.log2(step)
        rows_d[slot, 1] = jnp.exp2(decay[:, TILE - 1 : TILE] - decay) * step
        cols_d[slot] = decay.T

    sums(0)

    def advance(slot, _):
        for copy in fetches(slot):
            copy.wait()
        live_rows = row_ids + slot * TILE < length
        shared = []
        for g in range(groups):
            b = bs[slot, :, g * N : (g + 1) * N]
            c = cs[slot, :, g * N : (g + 1) * N]
            scores = lax.dot_general(c, b, (((1,), (1,)), ((), ())), preferred_element_type=F32)
            scores = jnp.where(row_ids >= col_ids, scores, 0.0)
            shared.append((c, scores, b.astype(F32).T))
        offset = rows_d[slot, 0]
        to_end = rows_d[slot, 1]
        decay_t = cols_d[slot]
        for pair in range(heads // 2):
            cols = pl.ds(pair * TILE, TILE)
            c, scores, b_t = shared[2 * pair // per_group]
            mix, weighted, decay_col = [], [], []
            for h in (2 * pair, 2 * pair + 1):
                column = jnp.broadcast_to(decay_t[:, h : h + 1], (TILE, TILE))
                gap = jnp.minimum(column - offset[h : h + 1, :], CEILING)
                mix.append((jnp.exp2(gap) * scores).astype(BF16))
                weighted.append((b_t * to_end[h : h + 1, :]).astype(BF16))
                decay_col.append(column)
            lhs = jnp.concatenate(
                [jnp.concatenate(mix, axis=1), jnp.concatenate(weighted, axis=1)], axis=0
            )
            x = xs[slot, :, cols]
            zero = jnp.zeros_like(x)
            rhs = jnp.concatenate([jnp.where(left, x, zero), jnp.where(left, zero, x)], axis=0)
            both = jnp.dot(lhs, rhs, preferred_element_type=F32)
            held = state[:, cols]
            carried = jnp.dot(c, held.astype(BF16), preferred_element_type=F32)
            growth = jnp.exp2(jnp.where(left, decay_col[0], decay_col[1]))
            first = start * per_group + 2 * pair
            skip = jnp.where(
                left[:1], gain_ref[1, first : first + 1, :], gain_ref[1, first + 1 : first + 2, :]
            )
            result = both[:TILE] + carried * growth + skip * x.astype(F32)
            outs[slot, :, cols] = jnp.where(live_rows, result, 0.0).astype(BF16)
            shrink = growth[TILE - 1 : TILE, :]
            state[:, cols] = shrink * held + both[TILE:]
        sums(jnp.minimum(slot + 1, SLOTS - 1))

        @pl.when(slot < W - before)
        def _():
            for copy in to_layer(slot):
                copy.start()

        @pl.when(slot >= W - before)
        def _():
            for copy in to_tail(slot):
                copy.start()

        return 0

    lax.fori_loop(0, filled, advance, 0)
    last = pltpu.make_async_copy(state, state_hbm.at[:, wide], end_sems.at[1])
    last.start()

    def drain(slot, _):
        @pl.when(slot < W - before)
        def _():
            for copy in to_layer(slot):
                copy.wait()

        @pl.when(slot >= W - before)
        def _():
            for copy in to_tail(slot):
                copy.wait()

        return 0

    lax.fori_loop(0, filled, drain, 0)
    last.wait()


def run_groups(start, groups, total, meta, x_rows, b_rows, c_rows, time_step, gains, carry):
    head_count = time_step.shape[0]
    heads = head_count // total * groups
    columns = x_rows.shape[1]
    width = columns // head_count
    part = columns // total
    span = part * groups
    whole = pl.BlockSpec(memory_space=pl.ANY)
    in_specs = [whole] * 4 + [pl.BlockSpec(memory_space=pltpu.VMEM)]
    aliases = {}
    extra = ()
    if carry is not None:
        extra = carry
        in_specs += [whole] * 2
        aliases = {6: 0, 7: 1}
    grid_spec = pltpu.PrefetchScalarGridSpec(
        num_scalar_prefetch=1,
        grid=(),
        in_specs=in_specs,
        out_specs=[whole] * (2 + groups),
        scratch_shapes=[
            pltpu.VMEM((SLOTS, TILE, span), BF16),
            pltpu.VMEM((SLOTS, TILE, groups * N), BF16),
            pltpu.VMEM((SLOTS, TILE, groups * N), BF16),
            pltpu.VMEM((heads, SLOTS * TILE), BF16),
            pltpu.VMEM((SLOTS, TILE, span), BF16),
            pltpu.VMEM((N, span), F32),
            pltpu.VMEM((SLOTS, 2, heads, TILE), F32),
            pltpu.VMEM((SLOTS, TILE, heads), F32),
            pltpu.SemaphoreType.DMA((3, SLOTS)),
            pltpu.SemaphoreType.DMA((1 + groups, SLOTS)),
            pltpu.SemaphoreType.DMA((2,)),
        ],
    )
    layer, state, *tails = pl.pallas_call(
        lambda *refs: scan_kernel(start, groups, heads, width, *refs),
        grid_spec=grid_spec,
        out_shape=[
            jax.ShapeDtypeStruct((W * TILE, columns), BF16),
            jax.ShapeDtypeStruct((N, columns), F32),
        ]
        + [jax.ShapeDtypeStruct((TAIL * TILE, part), BF16)] * groups,
        input_output_aliases=aliases,
        compiler_params=pltpu.CompilerParams(vmem_limit_bytes=VMEM),
        cost_estimate=pl.CostEstimate(flops=3 * 10**10, bytes_accessed=8 * 10**6, transcendentals=0),
    )(meta, x_rows, b_rows, c_rows, time_step, gains, *extra)
    return tails, (layer, state)


def finish(meta, state, token):
    columns = state.shape[1]
    span = columns // 4

    def kernel(meta, state_ref, token, kept_ref, send_ref):
        for part in range(span // TILE):
            cols = pl.ds(part * TILE, TILE)
            final = state_ref[:, cols].T
            kept_ref[cols, :] = jnp.where(meta[3] == 1, final, 0.0)
            send_ref[cols, :] = final.astype(BF16)

    return pl.pallas_call(
        kernel,
        grid_spec=pltpu.PrefetchScalarGridSpec(
            num_scalar_prefetch=1,
            grid=(columns // span,),
            in_specs=[
                pl.BlockSpec((N, span), lambda i, m: (0, i)),
                pl.BlockSpec(memory_space=pltpu.SMEM),
            ],
            out_specs=[pl.BlockSpec((span, N), lambda i, m: (i, 0))] * 2,
        ),
        out_shape=[
            jax.ShapeDtypeStruct((columns, N), F32),
            jax.ShapeDtypeStruct((columns, N), BF16),
        ],
        compiler_params=pltpu.CompilerParams(vmem_limit_bytes=VMEM),
        cost_estimate=pl.CostEstimate(flops=3 * 10**10, bytes_accessed=5 * 10**6, transcendentals=0),
    )(meta, state, token)


def place_chunk(chunk, meta, moved, layer, after=()):
    span = moved.shape[1]

    def kernel(meta, moved_ref, *rest):
        layer_ref, token, sems = rest[-3:]
        token[0] = 0
        copies = []
        for j in range(TAIL):
            rows = pl.ds(j * TILE, TILE)
            target = layer_ref.at[rows, pl.ds(chunk * span, span)]
            copies.append(pltpu.make_async_copy(moved_ref.at[rows, :], target, sems.at[j]))
        for j in range(TAIL):
            pl.when(j < meta[2])(copies[j].start)
        for j in range(TAIL):
            pl.when(j < meta[2])(copies[j].wait)

    return pl.pallas_call(
        kernel,
        grid_spec=pltpu.PrefetchScalarGridSpec(
            num_scalar_prefetch=1,
            grid=(),
            in_specs=[pl.BlockSpec(memory_space=pltpu.VMEM)]
            + [pl.BlockSpec(memory_space=pl.ANY)]
            + [pl.BlockSpec(memory_space=pltpu.SMEM)] * len(after),
            out_specs=[pl.BlockSpec(memory_space=pl.ANY), pl.BlockSpec(memory_space=pltpu.SMEM)],
            scratch_shapes=[pltpu.SemaphoreType.DMA((TAIL,))],
        ),
        out_shape=[
            jax.ShapeDtypeStruct(layer.shape, layer.dtype),
            jax.ShapeDtypeStruct((1,), jnp.int32),
        ],
        input_output_aliases={2: 0},
        compiler_params=pltpu.CompilerParams(vmem_limit_bytes=VMEM // 8),
        cost_estimate=pl.CostEstimate(flops=3 * 10**10, bytes_accessed=2 * 10**6, transcendentals=0),
    )(meta, moved, layer, *after)


def place_states(source, arrived):
    _, heads, width, entries = arrived.shape

    def kernel(source, arrived_ref, decode_hbm, token, held, sems):
        copies = []
        for c in range(DCAP):
            request = source[c]
            value = arrived_ref[jnp.maximum(request, 0)].astype(F32)
            held[c] = jnp.where(request >= 0, value, 0.0)
            copies.append(pltpu.make_async_copy(held.at[c], decode_hbm.at[:, c], sems.at[c]))
            copies[c].start()
        token[0] = 0
        for copy in copies:
            copy.wait()

    return pl.pallas_call(
        kernel,
        grid_spec=pltpu.PrefetchScalarGridSpec(
            num_scalar_prefetch=1,
            grid=(),
            in_specs=[pl.BlockSpec(memory_space=pltpu.VMEM)],
            out_specs=[pl.BlockSpec(memory_space=pl.ANY), pl.BlockSpec(memory_space=pltpu.SMEM)],
            scratch_shapes=[
                pltpu.VMEM((DCAP, heads, width, entries), F32),
                pltpu.SemaphoreType.DMA((DCAP,)),
            ],
        ),
        out_shape=[
            jax.ShapeDtypeStruct((heads, DCAP, width, entries), F32),
            jax.ShapeDtypeStruct((1,), jnp.int32),
        ],
        compiler_params=pltpu.CompilerParams(vmem_limit_bytes=VMEM),
        cost_estimate=pl.CostEstimate(flops=0, bytes_accessed=5 * 10**6, transcendentals=0),
    )(source, arrived)


def body(
    x_rows,
    b_rows,
    c_rows,
    time_step,
    decay_log,
    skip_gain,
    prompt_lengths,
    block_lists,
    decode_slot,
    staying,
):
    head_count = decay_log.shape[0]
    columns = x_rows.shape[1]
    width = columns // head_count
    chunks = b_rows.shape[1] // N
    req_count = lax.axis_size("req")
    meta, source, gains = prepare(prompt_lengths, decode_slot, staying, decay_log, skip_gain)
    moved = []
    carry = None
    for start, groups in ((0, chunks // 2), (chunks // 2, chunks - chunks // 2)):
        tails, carry = run_groups(
            start, groups, chunks, meta, x_rows, b_rows, c_rows, time_step, gains, carry
        )
        moved += [shifted(tail, "req", 1) for tail in tails]
    layer, state = carry
    token = meta[:1]
    for turn, chunk in enumerate(range(chunks)):
        if turn == 0:
            kept, send = finish(meta, state, token)
            pieces = send.reshape(DEC_REQ, head_count // DEC_REQ, width, N)
            groups = req_count // DEC_REQ
            outgoing = jnp.concatenate([pieces] * groups, axis=0) if groups > 1 else pieces
            arrived = lax.all_to_all(outgoing, "req", split_axis=0, concat_axis=0, tiled=True)
        if turn == 2:
            decoded, token = place_states(source, arrived)
        after = (token,) if turn == 2 else ()
        layer, token = place_chunk(chunk, meta, moved[chunk], layer, after)
    return (layer, kept.reshape(1, head_count, width, N), decoded[None, None])


def solution(mesh):
    placed = (
        P(("grp", "req"), "head"),
        P(("grp", "req"), "head"),
        P(("grp", "req"), "head"),
        P("head", ("grp", "req")),
        P("head"),
        P("head"),
        P("grp"),
        P("grp", None),
        P("grp"),
        P("grp"),
    )
    return jax.shard_map(
        body,
        mesh=mesh,
        in_specs=placed,
        out_specs=(
            P(("grp", "req"), "head"),
            P(("grp", "req"), "head", None, None),
            P(("grp", "req"), "head", None, None, None, None),
        ),
        check_vma=False,
    )
```

```python
import math

import jax
import jax.numpy as jnp
from jax import lax
from jax.experimental import pallas as pl
from jax.experimental.pallas import tpu as pltpu
from jax.sharding import PartitionSpec as P

N = 128
TILE = 128
W = 6
TAIL = W - 1
DCAP = 12
DEC_REQ = 8
SLOTS = 11
VMEM = 58 * 1024 * 1024
CEILING = 64.0
LOG2E = math.log2(math.e)
F32 = jnp.float32
BF16 = jnp.bfloat16


def shifted(block, axis, distance):
    devices = range(lax.axis_size(axis))
    route = [(i - distance, i) for i in devices if i - distance in devices]
    return lax.ppermute(block, axis, route)


def prepare(prompt_lengths, decode_slot, staying, decay_log, skip_gain):
    req_count = prompt_lengths.shape[0]
    head_count = decay_log.shape[0]

    def kernel(lengths, slots, stays, decay_ref, skip_ref, meta, source, gains):
        device = lax.axis_index("req")
        blocks = lambda r: (lengths[r] + TILE - 1) // TILE
        before = jnp.int32(0)
        for r in range(req_count):
            before += jnp.where(r < device, blocks(r) - W, 0)
        meta[0] = lengths[device]
        meta[1] = blocks(device)
        meta[2] = before
        meta[3] = stays[device]
        first = (device // DEC_REQ) * DCAP
        for c in range(DCAP):
            found = jnp.int32(-1)
            for r in range(req_count):
                found = jnp.where((slots[r] == first + c) & (stays[r] == 0), r, found)
            source[c] = found
        spread = lambda row: jnp.broadcast_to(row, (TILE, head_count)).T
        gains[0] = spread(-LOG2E * jnp.exp(decay_ref[...]))
        gains[1] = spread(skip_ref[...])

    smem = pl.BlockSpec(memory_space=pltpu.SMEM)
    vmem = pl.BlockSpec(memory_space=pltpu.VMEM)
    return pl.pallas_call(
        kernel,
        in_specs=[smem, smem, smem, vmem, vmem],
        out_specs=[smem, smem, vmem],
        out_shape=[
            jax.ShapeDtypeStruct((4,), jnp.int32),
            jax.ShapeDtypeStruct((DCAP,), jnp.int32),
            jax.ShapeDtypeStruct((2, head_count, TILE), F32),
        ],
    )(prompt_lengths, decode_slot, staying, decay_log[None, :], skip_gain[None, :])


def scan_kernel(start, groups, heads, width, meta, x_hbm, b_hbm, c_hbm, dt_hbm, gain_ref, *rest):
    outputs = rest[-13 - groups : -11]
    layer_hbm, state_hbm = outputs[:2]
    tails_hbm = outputs[2:]
    (xs, bs, cs, dts, outs, state, rows_d, cols_d, in_sems, out_sems, end_sems) = rest[-11:]
    length, filled, before = meta[0], meta[1], meta[2]
    span = xs.shape[2]
    part = span // groups
    per_group = heads // groups
    wide = pl.ds(start * part, span)
    narrow = pl.ds(start * N, groups * N)

    def block(slot):
        return pl.ds(pl.multiple_of(slot * TILE, TILE), TILE)

    def fetches(slot):
        return [
            pltpu.make_async_copy(c_hbm.at[block(slot), narrow], cs.at[slot], in_sems.at[0, slot]),
            pltpu.make_async_copy(b_hbm.at[block(slot), narrow], bs.at[slot], in_sems.at[1, slot]),
            pltpu.make_async_copy(x_hbm.at[block(slot), wide], xs.at[slot], in_sems.at[2, slot]),
        ]

    def to_layer(slot):
        target = layer_hbm.at[block(slot + before), wide]
        return [pltpu.make_async_copy(outs.at[slot], target, out_sems.at[0, slot])]

    def to_tail(slot):
        copies = []
        for g in range(groups):
            target = tails_hbm[g].at[block(slot - W + before)]
            source = outs.at[slot, :, pl.ds(g * part, part)]
            copies.append(pltpu.make_async_copy(source, target, out_sems.at[1 + g, slot]))
        return copies

    steps = pltpu.make_async_copy(
        dt_hbm.at[pl.ds(start * per_group, heads), :], dts, end_sems.at[0]
    )
    steps.start()
    for slot in range(SLOTS):

        @pl.when(slot < filled)
        def _():
            for copy in fetches(slot):
                copy.start()

    state[...] = jnp.zeros_like(state)
    row_ids = lax.broadcasted_iota(jnp.int32, (TILE, TILE), 0)
    col_ids = lax.broadcasted_iota(jnp.int32, (TILE, TILE), 1)
    left = col_ids < width
    upper = jnp.where(row_ids <= col_ids, 1.0, 0.0).astype(BF16)
    rate = gain_ref[0, start * per_group : start * per_group + heads, :]
    steps.wait()

    def sums(slot):
        live = lax.broadcasted_iota(jnp.int32, (1, TILE), 1) + slot * TILE < length
        step = jnp.where(live, dts[:, block(slot)].astype(F32), 0.0)
        total = jnp.dot(step.astype(BF16), upper, preferred_element_type=F32)
        decay = total * rate
        rows_d[slot, 0] = decay - jnp.log2(step)
        rows_d[slot, 1] = jnp.exp2(decay[:, TILE - 1 : TILE] - decay) * step
        cols_d[slot] = decay.T

    sums(0)

    def advance(slot, _):
        for copy in fetches(slot):
            copy.wait()
        live_rows = row_ids + slot * TILE < length
        shared = []
        for g in range(groups):
            b = bs[slot, :, g * N : (g + 1) * N]
            c = cs[slot, :, g * N : (g + 1) * N]
            scores = lax.dot_general(c, b, (((1,), (1,)), ((), ())), preferred_element_type=F32)
            scores = jnp.where(row_ids >= col_ids, scores, 0.0)
            held = state[:, g * part : (g + 1) * part]
            read = jnp.dot(c, held.astype(BF16), preferred_element_type=F32)
            shared.append((scores, b.astype(F32).T, read))
        offset = rows_d[slot, 0]
        to_end = rows_d[slot, 1]
        decay_t = cols_d[slot]
        for pair in range(heads // 2):
            cols = pl.ds(pair * TILE, TILE)
            scores, b_t, read = shared[2 * pair // per_group]
            mix, weighted, decay_col = [], [], []
            for h in (2 * pair, 2 * pair + 1):
                column = jnp.broadcast_to(decay_t[:, h : h + 1], (TILE, TILE))
                gap = jnp.minimum(column - offset[h : h + 1, :], CEILING)
                mix.append((jnp.exp2(gap) * scores).astype(BF16))
                weighted.append((b_t * to_end[h : h + 1, :]).astype(BF16))
                decay_col.append(column)
            lhs = jnp.concatenate(
                [jnp.concatenate(mix, axis=1), jnp.concatenate(weighted, axis=1)], axis=0
            )
            x = xs[slot, :, cols]
            zero = jnp.zeros_like(x)
            rhs = jnp.concatenate([jnp.where(left, x, zero), jnp.where(left, zero, x)], axis=0)
            both = jnp.dot(lhs, rhs, preferred_element_type=F32)
            held = state[:, cols]
            lane = pair * TILE % part
            carried = read[:, lane : lane + TILE]
            growth = jnp.exp2(jnp.where(left, decay_col[0], decay_col[1]))
            first = start * per_group + 2 * pair
            skip = jnp.where(
                left[:1], gain_ref[1, first : first + 1, :], gain_ref[1, first + 1 : first + 2, :]
            )
            result = both[:TILE] + carried * growth + skip * x.astype(F32)
            outs[slot, :, cols] = jnp.where(live_rows, result, 0.0).astype(BF16)
            shrink = growth[TILE - 1 : TILE, :]
            state[:, cols] = shrink * held + both[TILE:]
        sums(jnp.minimum(slot + 1, SLOTS - 1))

        @pl.when(slot < W - before)
        def _():
            for copy in to_layer(slot):
                copy.start()

        @pl.when(slot >= W - before)
        def _():
            for copy in to_tail(slot):
                copy.start()

        return 0

    lax.fori_loop(0, filled, advance, 0)
    last = pltpu.make_async_copy(state, state_hbm.at[:, wide], end_sems.at[1])
    last.start()

    def drain(slot, _):
        @pl.when(slot < W - before)
        def _():
            for copy in to_layer(slot):
                copy.wait()

        @pl.when(slot >= W - before)
        def _():
            for copy in to_tail(slot):
                copy.wait()

        return 0

    lax.fori_loop(0, filled, drain, 0)
    last.wait()


def run_groups(start, groups, total, meta, x_rows, b_rows, c_rows, time_step, gains, carry):
    head_count = time_step.shape[0]
    heads = head_count // total * groups
    columns = x_rows.shape[1]
    width = columns // head_count
    part = columns // total
    span = part * groups
    whole = pl.BlockSpec(memory_space=pl.ANY)
    in_specs = [whole] * 4 + [pl.BlockSpec(memory_space=pltpu.VMEM)]
    aliases = {}
    extra = ()
    if carry is not None:
        extra = carry
        in_specs += [whole] * 2
        aliases = {6: 0, 7: 1}
    grid_spec = pltpu.PrefetchScalarGridSpec(
        num_scalar_prefetch=1,
        grid=(),
        in_specs=in_specs,
        out_specs=[whole] * (2 + groups),
        scratch_shapes=[
            pltpu.VMEM((SLOTS, TILE, span), BF16),
            pltpu.VMEM((SLOTS, TILE, groups * N), BF16),
            pltpu.VMEM((SLOTS, TILE, groups * N), BF16),
            pltpu.VMEM((heads, SLOTS * TILE), BF16),
            pltpu.VMEM((SLOTS, TILE, span), BF16),
            pltpu.VMEM((N, span), F32),
            pltpu.VMEM((SLOTS, 2, heads, TILE), F32),
            pltpu.VMEM((SLOTS, TILE, heads), F32),
            pltpu.SemaphoreType.DMA((3, SLOTS)),
            pltpu.SemaphoreType.DMA((1 + groups, SLOTS)),
            pltpu.SemaphoreType.DMA((2,)),
        ],
    )
    layer, state, *tails = pl.pallas_call(
        lambda *refs: scan_kernel(start, groups, heads, width, *refs),
        grid_spec=grid_spec,
        out_shape=[
            jax.ShapeDtypeStruct((W * TILE, columns), BF16),
            jax.ShapeDtypeStruct((N, columns), F32),
        ]
        + [jax.ShapeDtypeStruct((TAIL * TILE, part), BF16)] * groups,
        input_output_aliases=aliases,
        compiler_params=pltpu.CompilerParams(vmem_limit_bytes=VMEM),
        cost_estimate=pl.CostEstimate(flops=3 * 10**10, bytes_accessed=8 * 10**6, transcendentals=0),
    )(meta, x_rows, b_rows, c_rows, time_step, gains, *extra)
    return tails, (layer, state)


def finish(meta, state, token):
    columns = state.shape[1]
    span = columns // 4

    def kernel(meta, state_ref, token, kept_ref, send_ref):
        for part in range(span // TILE):
            cols = pl.ds(part * TILE, TILE)
            final = state_ref[:, cols].T
            kept_ref[cols, :] = jnp.where(meta[3] == 1, final, 0.0)
            send_ref[cols, :] = final.astype(BF16)

    return pl.pallas_call(
        kernel,
        grid_spec=pltpu.PrefetchScalarGridSpec(
            num_scalar_prefetch=1,
            grid=(columns // span,),
            in_specs=[
                pl.BlockSpec((N, span), lambda i, m: (0, i)),
                pl.BlockSpec(memory_space=pltpu.SMEM),
            ],
            out_specs=[pl.BlockSpec((span, N), lambda i, m: (i, 0))] * 2,
        ),
        out_shape=[
            jax.ShapeDtypeStruct((columns, N), F32),
            jax.ShapeDtypeStruct((columns, N), BF16),
        ],
        compiler_params=pltpu.CompilerParams(vmem_limit_bytes=VMEM),
        cost_estimate=pl.CostEstimate(flops=3 * 10**10, bytes_accessed=5 * 10**6, transcendentals=0),
    )(meta, state, token)


def place_chunk(chunk, meta, moved, layer, after=()):
    span = moved.shape[1]

    def kernel(meta, moved_ref, *rest):
        layer_ref, token, sems = rest[-3:]
        token[0] = 0
        copies = []
        for j in range(TAIL):
            rows = pl.ds(j * TILE, TILE)
            target = layer_ref.at[rows, pl.ds(chunk * span, span)]
            copies.append(pltpu.make_async_copy(moved_ref.at[rows, :], target, sems.at[j]))
        for j in range(TAIL):
            pl.when(j < meta[2])(copies[j].start)
        for j in range(TAIL):
            pl.when(j < meta[2])(copies[j].wait)

    return pl.pallas_call(
        kernel,
        grid_spec=pltpu.PrefetchScalarGridSpec(
            num_scalar_prefetch=1,
            grid=(),
            in_specs=[pl.BlockSpec(memory_space=pltpu.VMEM)]
            + [pl.BlockSpec(memory_space=pl.ANY)]
            + [pl.BlockSpec(memory_space=pltpu.SMEM)] * len(after),
            out_specs=[pl.BlockSpec(memory_space=pl.ANY), pl.BlockSpec(memory_space=pltpu.SMEM)],
            scratch_shapes=[pltpu.SemaphoreType.DMA((TAIL,))],
        ),
        out_shape=[
            jax.ShapeDtypeStruct(layer.shape, layer.dtype),
            jax.ShapeDtypeStruct((1,), jnp.int32),
        ],
        input_output_aliases={2: 0},
        compiler_params=pltpu.CompilerParams(vmem_limit_bytes=VMEM // 8),
        cost_estimate=pl.CostEstimate(flops=3 * 10**10, bytes_accessed=2 * 10**6, transcendentals=0),
    )(meta, moved, layer, *after)


def place_states(source, arrived):
    _, heads, width, entries = arrived.shape

    def kernel(source, arrived_ref, decode_hbm, token, held, sems):
        copies = []
        for c in range(DCAP):
            request = source[c]
            value = arrived_ref[jnp.maximum(request, 0)].astype(F32)
            held[c] = jnp.where(request >= 0, value, 0.0)
            copies.append(pltpu.make_async_copy(held.at[c], decode_hbm.at[:, c], sems.at[c]))
            copies[c].start()
        token[0] = 0
        for copy in copies:
            copy.wait()

    return pl.pallas_call(
        kernel,
        grid_spec=pltpu.PrefetchScalarGridSpec(
            num_scalar_prefetch=1,
            grid=(),
            in_specs=[pl.BlockSpec(memory_space=pltpu.VMEM)],
            out_specs=[pl.BlockSpec(memory_space=pl.ANY), pl.BlockSpec(memory_space=pltpu.SMEM)],
            scratch_shapes=[
                pltpu.VMEM((DCAP, heads, width, entries), F32),
                pltpu.SemaphoreType.DMA((DCAP,)),
            ],
        ),
        out_shape=[
            jax.ShapeDtypeStruct((heads, DCAP, width, entries), F32),
            jax.ShapeDtypeStruct((1,), jnp.int32),
        ],
        compiler_params=pltpu.CompilerParams(vmem_limit_bytes=VMEM),
        cost_estimate=pl.CostEstimate(flops=0, bytes_accessed=5 * 10**6, transcendentals=0),
    )(source, arrived)


def body(
    x_rows,
    b_rows,
    c_rows,
    time_step,
    decay_log,
    skip_gain,
    prompt_lengths,
    block_lists,
    decode_slot,
    staying,
):
    head_count = decay_log.shape[0]
    columns = x_rows.shape[1]
    width = columns // head_count
    chunks = b_rows.shape[1] // N
    req_count = lax.axis_size("req")
    meta, source, gains = prepare(prompt_lengths, decode_slot, staying, decay_log, skip_gain)
    moved = []
    carry = None
    for start, groups in ((0, 1), (1, 1), (2, chunks - 2)):
        tails, carry = run_groups(
            start, groups, chunks, meta, x_rows, b_rows, c_rows, time_step, gains, carry
        )
        moved += [shifted(tail, "req", 1) for tail in tails]
    layer, state = carry
    token = meta[:1]
    for turn, chunk in enumerate(range(chunks)):
        if turn == 0:
            kept, send = finish(meta, state, token)
            pieces = send.reshape(DEC_REQ, head_count // DEC_REQ, width, N)
            groups = req_count // DEC_REQ
            outgoing = jnp.concatenate([pieces] * groups, axis=0) if groups > 1 else pieces
            arrived = lax.all_to_all(outgoing, "req", split_axis=0, concat_axis=0, tiled=True)
        if turn == 2:
            decoded, token = place_states(source, arrived)
        after = (token,) if turn == 2 else ()
        layer, token = place_chunk(chunk, meta, moved[chunk], layer, after)
    return (layer, kept.reshape(1, head_count, width, N), decoded[None, None])


def solution(mesh):
    placed = (
        P(("grp", "req"), "head"),
        P(("grp", "req"), "head"),
        P(("grp", "req"), "head"),
        P("head", ("grp", "req")),
        P("head"),
        P("head"),
        P("grp"),
        P("grp", None),
        P("grp"),
        P("grp"),
    )
    return jax.shard_map(
        body,
        mesh=mesh,
        in_specs=placed,
        out_specs=(
            P(("grp", "req"), "head"),
            P(("grp", "req"), "head", None, None),
            P(("grp", "req"), "head", None, None, None, None),
        ),
        check_vma=False,
    )
```

```python
import math

import jax
import jax.numpy as jnp
from jax import lax
from jax.experimental import pallas as pl
from jax.experimental.pallas import tpu as pltpu
from jax.sharding import PartitionSpec as P

N = 128
TILE = 128
W = 6
TAIL = W - 1
STRIP = 32
DCAP = 12
DEC_REQ = 8
SLOTS = 11
VMEM = 58 * 1024 * 1024
CEILING = 64.0
LOG2E = math.log2(math.e)
F32 = jnp.float32
BF16 = jnp.bfloat16


def shifted(block, axis, distance):
    devices = range(lax.axis_size(axis))
    route = [(i - distance, i) for i in devices if i - distance in devices]
    return lax.ppermute(block, axis, route)


def prepare(prompt_lengths, decode_slot, staying, decay_log, skip_gain):
    req_count = prompt_lengths.shape[0]
    head_count = decay_log.shape[0]

    def kernel(lengths, slots, stays, decay_ref, skip_ref, meta, source, gains):
        device = lax.axis_index("req")
        blocks = lambda r: (lengths[r] + TILE - 1) // TILE
        before = jnp.int32(0)
        for r in range(req_count):
            before += jnp.where(r < device, blocks(r) - W, 0)
        meta[0] = lengths[device]
        meta[1] = blocks(device)
        meta[2] = before
        meta[3] = stays[device]
        first = (device // DEC_REQ) * DCAP
        for c in range(DCAP):
            found = jnp.int32(-1)
            for r in range(req_count):
                found = jnp.where((slots[r] == first + c) & (stays[r] == 0), r, found)
            source[c] = found
        spread = lambda row: jnp.broadcast_to(row, (TILE, head_count)).T
        gains[0] = spread(-LOG2E * jnp.exp(decay_ref[...]))
        gains[1] = spread(skip_ref[...])

    smem = pl.BlockSpec(memory_space=pltpu.SMEM)
    vmem = pl.BlockSpec(memory_space=pltpu.VMEM)
    return pl.pallas_call(
        kernel,
        in_specs=[smem, smem, smem, vmem, vmem],
        out_specs=[smem, smem, vmem],
        out_shape=[
            jax.ShapeDtypeStruct((4,), jnp.int32),
            jax.ShapeDtypeStruct((DCAP,), jnp.int32),
            jax.ShapeDtypeStruct((2, head_count, TILE), F32),
        ],
    )(prompt_lengths, decode_slot, staying, decay_log[None, :], skip_gain[None, :])


def scan_kernel(start, groups, heads, width, meta, x_hbm, b_hbm, c_hbm, dt_hbm, gain_ref, *rest):
    outputs = rest[-13 - groups : -11]
    layer_hbm, state_hbm = outputs[:2]
    tails_hbm = outputs[2:]
    (xs, bs, cs, dts, outs, state, rows_d, cols_d, in_sems, out_sems, end_sems) = rest[-11:]
    length, filled, before = meta[0], meta[1], meta[2]
    span = xs.shape[2]
    part = span // groups
    per_group = heads // groups
    wide = pl.ds(start * part, span)
    narrow = pl.ds(start * N, groups * N)

    def block(slot):
        return pl.ds(pl.multiple_of(slot * TILE, TILE), TILE)

    def fetches(slot):
        return [
            pltpu.make_async_copy(c_hbm.at[block(slot), narrow], cs.at[slot], in_sems.at[0, slot]),
            pltpu.make_async_copy(b_hbm.at[block(slot), narrow], bs.at[slot], in_sems.at[1, slot]),
            pltpu.make_async_copy(x_hbm.at[block(slot), wide], xs.at[slot], in_sems.at[2, slot]),
        ]

    def to_layer(slot):
        target = layer_hbm.at[block(slot + before), wide]
        return [pltpu.make_async_copy(outs.at[slot], target, out_sems.at[0, slot])]

    def to_tail(slot):
        copies = []
        for g in range(groups):
            target = tails_hbm[g].at[block(slot - W + before)]
            source = outs.at[slot, :, pl.ds(g * part, part)]
            copies.append(pltpu.make_async_copy(source, target, out_sems.at[1 + g, slot]))
        return copies

    steps = pltpu.make_async_copy(
        dt_hbm.at[pl.ds(start * per_group, heads), :], dts, end_sems.at[0]
    )
    steps.start()
    for slot in range(SLOTS):

        @pl.when(slot < filled)
        def _():
            for copy in fetches(slot):
                copy.start()

    state[...] = jnp.zeros_like(state)
    row_ids = lax.broadcasted_iota(jnp.int32, (TILE, TILE), 0)
    col_ids = lax.broadcasted_iota(jnp.int32, (TILE, TILE), 1)
    left = col_ids < width
    upper = jnp.where(row_ids <= col_ids, 1.0, 0.0).astype(BF16)
    rate = gain_ref[0, start * per_group : start * per_group + heads, :]
    steps.wait()

    def sums(slot):
        live = lax.broadcasted_iota(jnp.int32, (1, TILE), 1) + slot * TILE < length
        step = jnp.where(live, dts[:, block(slot)].astype(F32), 0.0)
        total = jnp.dot(step.astype(BF16), upper, preferred_element_type=F32)
        decay = total * rate
        rows_d[slot, 0] = decay - jnp.log2(step)
        rows_d[slot, 1] = jnp.exp2(decay[:, TILE - 1 : TILE] - decay) * step
        cols_d[slot] = decay.T

    sums(0)

    def advance(slot, _):
        for copy in fetches(slot):
            copy.wait()
        live_rows = row_ids + slot * TILE < length
        shared = []
        for g in range(groups):
            b = bs[slot, :, g * N : (g + 1) * N]
            c = cs[slot, :, g * N : (g + 1) * N]
            scores = lax.dot_general(c, b, (((1,), (1,)), ((), ())), preferred_element_type=F32)
            scores = jnp.where(row_ids >= col_ids, scores, 0.0)
            held = state[:, g * part : (g + 1) * part]
            read = jnp.dot(c, held.astype(BF16), preferred_element_type=F32)
            shared.append((scores, b.astype(F32).T, read))
        offset = rows_d[slot, 0]
        to_end = rows_d[slot, 1]
        decay_t = cols_d[slot]
        for pair in range(heads // 2):
            cols = pl.ds(pair * TILE, TILE)
            scores, b_t, read = shared[2 * pair // per_group]
            mix, weighted, decay_col = [], [], []
            for h in (2 * pair, 2 * pair + 1):
                column = jnp.broadcast_to(decay_t[:, h : h + 1], (TILE, TILE))
                gap = jnp.minimum(column - offset[h : h + 1, :], CEILING)
                mix.append((jnp.exp2(gap) * scores).astype(BF16))
                weighted.append((b_t * to_end[h : h + 1, :]).astype(BF16))
                decay_col.append(column)
            lhs = jnp.concatenate(
                [jnp.concatenate(mix, axis=1), jnp.concatenate(weighted, axis=1)], axis=0
            )
            x = xs[slot, :, cols]
            zero = jnp.zeros_like(x)
            rhs = jnp.concatenate([jnp.where(left, x, zero), jnp.where(left, zero, x)], axis=0)
            both = jnp.dot(lhs, rhs, preferred_element_type=F32)
            held = state[:, cols]
            lane = pair * TILE % part
            carried = read[:, lane : lane + TILE]
            growth = jnp.exp2(jnp.where(left, decay_col[0], decay_col[1]))
            first = start * per_group + 2 * pair
            skip = jnp.where(
                left[:1], gain_ref[1, first : first + 1, :], gain_ref[1, first + 1 : first + 2, :]
            )
            result = both[:TILE] + carried * growth + skip * x.astype(F32)
            outs[slot, :, cols] = jnp.where(live_rows, result, 0.0).astype(BF16)
            shrink = growth[TILE - 1 : TILE, :]
            state[:, cols] = shrink * held + both[TILE:]
        sums(jnp.minimum(slot + 1, SLOTS - 1))

        @pl.when(slot < W - before)
        def _():
            for copy in to_layer(slot):
                copy.start()

        @pl.when(slot >= W - before)
        def _():
            for copy in to_tail(slot):
                copy.start()

        return 0

    lax.fori_loop(0, filled, advance, 0)
    last = pltpu.make_async_copy(state, state_hbm.at[:, wide], end_sems.at[1])
    last.start()

    def drain(slot, _):
        @pl.when(slot < W - before)
        def _():
            for copy in to_layer(slot):
                copy.wait()

        @pl.when(slot >= W - before)
        def _():
            for copy in to_tail(slot):
                copy.wait()

        return 0

    lax.fori_loop(0, filled, drain, 0)
    last.wait()


def run_groups(start, groups, total, meta, x_rows, b_rows, c_rows, time_step, gains, carry):
    head_count = time_step.shape[0]
    heads = head_count // total * groups
    columns = x_rows.shape[1]
    width = columns // head_count
    part = columns // total
    span = part * groups
    whole = pl.BlockSpec(memory_space=pl.ANY)
    in_specs = [whole] * 4 + [pl.BlockSpec(memory_space=pltpu.VMEM)]
    aliases = {}
    extra = ()
    if carry is not None:
        extra = carry
        in_specs += [whole] * 2
        aliases = {6: 0, 7: 1}
    grid_spec = pltpu.PrefetchScalarGridSpec(
        num_scalar_prefetch=1,
        grid=(),
        in_specs=in_specs,
        out_specs=[whole] * (2 + groups),
        scratch_shapes=[
            pltpu.VMEM((SLOTS, TILE, span), BF16),
            pltpu.VMEM((SLOTS, TILE, groups * N), BF16),
            pltpu.VMEM((SLOTS, TILE, groups * N), BF16),
            pltpu.VMEM((heads, SLOTS * TILE), BF16),
            pltpu.VMEM((SLOTS, TILE, span), BF16),
            pltpu.VMEM((N, span), F32),
            pltpu.VMEM((SLOTS, 2, heads, TILE), F32),
            pltpu.VMEM((SLOTS, TILE, heads), F32),
            pltpu.SemaphoreType.DMA((3, SLOTS)),
            pltpu.SemaphoreType.DMA((1 + groups, SLOTS)),
            pltpu.SemaphoreType.DMA((2,)),
        ],
    )
    layer, state, *tails = pl.pallas_call(
        lambda *refs: scan_kernel(start, groups, heads, width, *refs),
        grid_spec=grid_spec,
        out_shape=[
            jax.ShapeDtypeStruct((W * TILE, columns), BF16),
            jax.ShapeDtypeStruct((N, columns), F32),
        ]
        + [jax.ShapeDtypeStruct((TAIL * TILE, part), BF16)] * groups,
        input_output_aliases=aliases,
        compiler_params=pltpu.CompilerParams(vmem_limit_bytes=VMEM),
        cost_estimate=pl.CostEstimate(flops=3 * 10**10, bytes_accessed=8 * 10**6, transcendentals=0),
    )(meta, x_rows, b_rows, c_rows, time_step, gains, *extra)
    return tails, (layer, state)


def finish(meta, state, token):
    columns = state.shape[1]
    span = columns // 8

    def kernel(meta, state_ref, token, kept_ref, send_ref):
        for part in range(span // TILE):
            cols = pl.ds(part * TILE, TILE)
            final = state_ref[:, cols].T
            kept_ref[cols, :] = jnp.where(meta[3] == 1, final, 0.0)
            send_ref[cols, :] = final.astype(BF16)

    return pl.pallas_call(
        kernel,
        grid_spec=pltpu.PrefetchScalarGridSpec(
            num_scalar_prefetch=1,
            grid=(columns // span,),
            in_specs=[
                pl.BlockSpec((N, span), lambda i, m: (0, i)),
                pl.BlockSpec(memory_space=pltpu.SMEM),
            ],
            out_specs=[pl.BlockSpec((span, N), lambda i, m: (i, 0))] * 2,
        ),
        out_shape=[
            jax.ShapeDtypeStruct((columns, N), F32),
            jax.ShapeDtypeStruct((columns, N), BF16),
        ],
        compiler_params=pltpu.CompilerParams(vmem_limit_bytes=VMEM),
        cost_estimate=pl.CostEstimate(flops=3 * 10**10, bytes_accessed=5 * 10**6, transcendentals=0),
    )(meta, state, token)


def place_chunk(chunk, meta, moved, layer, after=()):
    span = moved.shape[1]

    def kernel(meta, moved_ref, *rest):
        layer_ref, token, sems = rest[-3:]
        token[0] = 0
        copies = []
        strips = TILE // STRIP
        for j in range(TAIL * strips):
            rows = pl.ds(j * STRIP, STRIP)
            target = layer_ref.at[rows, pl.ds(chunk * span, span)]
            copies.append(pltpu.make_async_copy(moved_ref.at[rows, :], target, sems.at[j]))
        for j in range(TAIL):

            @pl.when(j < meta[2])
            def _():
                for copy in copies[j * strips : (j + 1) * strips]:
                    copy.start()

        for j in range(TAIL):

            @pl.when(j < meta[2])
            def _():
                for copy in copies[j * strips : (j + 1) * strips]:
                    copy.wait()

    return pl.pallas_call(
        kernel,
        grid_spec=pltpu.PrefetchScalarGridSpec(
            num_scalar_prefetch=1,
            grid=(),
            in_specs=[pl.BlockSpec(memory_space=pltpu.VMEM)]
            + [pl.BlockSpec(memory_space=pl.ANY)]
            + [pl.BlockSpec(memory_space=pltpu.SMEM)] * len(after),
            out_specs=[pl.BlockSpec(memory_space=pl.ANY), pl.BlockSpec(memory_space=pltpu.SMEM)],
            scratch_shapes=[pltpu.SemaphoreType.DMA((TAIL * TILE // STRIP,))],
        ),
        out_shape=[
            jax.ShapeDtypeStruct(layer.shape, layer.dtype),
            jax.ShapeDtypeStruct((1,), jnp.int32),
        ],
        input_output_aliases={2: 0},
        compiler_params=pltpu.CompilerParams(vmem_limit_bytes=VMEM // 8),
        cost_estimate=pl.CostEstimate(flops=3 * 10**10, bytes_accessed=2 * 10**6, transcendentals=0),
    )(meta, moved, layer, *after)


def place_states(source, arrived):
    _, heads, width, entries = arrived.shape

    def kernel(source, arrived_ref, decode_hbm, token, held, sems):
        copies = []
        for c in range(DCAP):
            request = source[c]
            value = arrived_ref[jnp.maximum(request, 0)].astype(F32)
            held[c] = jnp.where(request >= 0, value, 0.0)
            copies.append(pltpu.make_async_copy(held.at[c], decode_hbm.at[:, c], sems.at[c]))
            copies[c].start()
        token[0] = 0
        for copy in copies:
            copy.wait()

    return pl.pallas_call(
        kernel,
        grid_spec=pltpu.PrefetchScalarGridSpec(
            num_scalar_prefetch=1,
            grid=(),
            in_specs=[pl.BlockSpec(memory_space=pltpu.VMEM)],
            out_specs=[pl.BlockSpec(memory_space=pl.ANY), pl.BlockSpec(memory_space=pltpu.SMEM)],
            scratch_shapes=[
                pltpu.VMEM((DCAP, heads, width, entries), F32),
                pltpu.SemaphoreType.DMA((DCAP,)),
            ],
        ),
        out_shape=[
            jax.ShapeDtypeStruct((heads, DCAP, width, entries), F32),
            jax.ShapeDtypeStruct((1,), jnp.int32),
        ],
        compiler_params=pltpu.CompilerParams(vmem_limit_bytes=VMEM),
        cost_estimate=pl.CostEstimate(flops=0, bytes_accessed=5 * 10**6, transcendentals=0),
    )(source, arrived)


def body(
    x_rows,
    b_rows,
    c_rows,
    time_step,
    decay_log,
    skip_gain,
    prompt_lengths,
    block_lists,
    decode_slot,
    staying,
):
    head_count = decay_log.shape[0]
    columns = x_rows.shape[1]
    width = columns // head_count
    chunks = b_rows.shape[1] // N
    req_count = lax.axis_size("req")
    meta, source, gains = prepare(prompt_lengths, decode_slot, staying, decay_log, skip_gain)
    moved = []
    carry = None
    for start, groups in ((0, 1), (1, 1), (2, chunks - 2)):
        tails, carry = run_groups(
            start, groups, chunks, meta, x_rows, b_rows, c_rows, time_step, gains, carry
        )
        moved += [shifted(tail, "req", 1) for tail in tails]
    layer, state = carry
    token = meta[:1]
    for turn, chunk in enumerate(range(chunks)):
        if turn == 0:
            kept, send = finish(meta, state, token)
            pieces = send.reshape(DEC_REQ, head_count // DEC_REQ, width, N)
            groups = req_count // DEC_REQ
            outgoing = jnp.concatenate([pieces] * groups, axis=0) if groups > 1 else pieces
            arrived = lax.all_to_all(outgoing, "req", split_axis=0, concat_axis=0, tiled=True)
        if turn == 2:
            decoded, token = place_states(source, arrived)
        after = (token,) if turn == 2 else ()
        layer, token = place_chunk(chunk, meta, moved[chunk], layer, after)
    return (layer, kept.reshape(1, head_count, width, N), decoded[None, None])


def solution(mesh):
    placed = (
        P(("grp", "req"), "head"),
        P(("grp", "req"), "head"),
        P(("grp", "req"), "head"),
        P("head", ("grp", "req")),
        P("head"),
        P("head"),
        P("grp"),
        P("grp", None),
        P("grp"),
        P("grp"),
    )
    return jax.shard_map(
        body,
        mesh=mesh,
        in_specs=placed,
        out_specs=(
            P(("grp", "req"), "head"),
            P(("grp", "req"), "head", None, None),
            P(("grp", "req"), "head", None, None, None, None),
        ),
        check_vma=False,
    )
```
